512 devices in a mesh: ctx: 64 (over z, y), tp: 8 (over x, core).
Axes of the slice: x: 4, y: 4, z: 16, core: 2. Of those that a mesh axis runs over, the one named last changes fastest.
Arguments:
- queries: bfloat16 [16384, 4096], P('ctx', 'tp'), may hold values from -1.796875 to 1.796875
- keys: bfloat16 [16384, 4096], P('ctx', 'tp'), may hold values from -1.796875 to 1.796875
- values: bfloat16 [16384, 4096], P('ctx', 'tp'), may hold values from -6 to 6
- grad_out: bfloat16 [16384, 4096], P('ctx', 'tp'), may hold values from -6 to 6
- out_weight: bfloat16 [4096, 4096], P('ctx', 'tp'), may hold values from -0.09375 to 0.09375
Outputs:
- grad_queries: bfloat16 [16384, 4096], P('ctx', 'tp')
- grad_keys: bfloat16 [16384, 4096], P('ctx', 'tp')
- grad_values: bfloat16 [16384, 4096], P('ctx', 'tp')
The draws below stay inside these ranges and needn't reach their ends.
All inputs are finite; a program needn't handle non-finite values.
Results may differ from the reference program's by a relative error of at most 0.014.
Values may be sent and summed in bfloat16 or wider, within the bound.
No kernel may reach another device: no remote copies, remote signals or barrier semaphores. Data moves between devices by JAX's collectives and lax.ppermute only.
A program may use at most 128 MiB of HBM per device.

```python
import math
import jax
import jax.numpy as jnp
from jax import lax

H = 32
DH = 128
D = 4096
TOK_DEV = 256
SEQ = 16384


def shard_levels(key, shape, cuts, smallest, high):
    factor_of = 1.0
    for axis_at, shards_of in cuts:
        heights = jax.random.uniform(jax.random.fold_in(jax.random.fold_in(key, 6), axis_at), (shards_of,), jnp.float32, smallest / len(cuts), high / len(cuts))
        factor_of = factor_of * jnp.repeat(jnp.exp(heights), shape[axis_at] // shards_of).reshape((-1,) + (1,) * (len(shape) - 1 - axis_at))
    return factor_of


def centred(stream_key, extent, deviation, most, cuts=(), kind=jnp.bfloat16):
    factor_of = shard_levels(stream_key, extent, cuts, -0.22, 0.18) if cuts else 1.0
    values = jax.random.normal(stream_key, extent, jnp.float32) * deviation * factor_of
    return jnp.minimum(jnp.maximum(values, -most), most).astype(kind)


def setup_inputs(seed: int = 0) -> dict:
    splits = jax.random.split(jax.random.key(seed), 6)
    queries = centred(splits[0], (SEQ, H * DH), 0.3, 1.796875, ((0, 64), (1, 8)))
    keys = centred(splits[1], (SEQ, H * DH), 0.3, 1.796875, ((0, 64), (1, 8)))
    values = centred(splits[2], (SEQ, H * DH), 1.0, 6.0, ((0, 64), (1, 8)))
    grad_out = centred(splits[3], (SEQ, D), 1.0, 6.0, ((0, 64), (1, 8)))
    out_weight = centred(splits[4], (D, H * DH), D ** -0.5, 0.09375, ((0, 64), (1, 8)))
    return dict(queries=queries, keys=keys, values=values, grad_out=grad_out, out_weight=out_weight)


def reference(queries, keys, values, grad_out, out_weight):
    factor = 1.0 / math.sqrt(SEQ)
    blocks = SEQ // TOK_DEV
    positions = jnp.arange(TOK_DEV, dtype=jnp.int32)
    causal = positions[:, None] >= positions[None, :]

    def one_head(head_index):
        offset = (head_index * DH).astype(jnp.int32)
        weight_cols = lax.dynamic_slice_in_dim(out_weight, offset, DH, 1)
        head_grad = jnp.dot(grad_out, weight_cols, preferred_element_type=jnp.float32).astype(jnp.bfloat16)

        def split(array):
            part_cols = lax.dynamic_slice_in_dim(array, offset, DH, 1)
            return part_cols.reshape(blocks, TOK_DEV, DH).astype(jnp.float32)
        query_wide = split(queries)
        key_wide = split(keys)
        value_wide = split(values)
        grad_wide = head_grad.reshape(blocks, TOK_DEV, DH).astype(jnp.float32)
        key_state = jnp.einsum('bti,btj->bij', key_wide, value_wide)
        query_state = jnp.einsum('bti,btj->bij', query_wide, grad_wide)
        zero_state = jnp.zeros((1, DH, DH), jnp.float32)
        prefix = jnp.concatenate([zero_state, jnp.cumsum(key_state, axis=0)[:-1]], axis=0)
        inclusive = jnp.cumsum(query_state[::-1], axis=0)[::-1]
        suffix = jnp.concatenate([inclusive[1:], zero_state], axis=0)
        prefix = prefix.astype(jnp.bfloat16).astype(jnp.float32)
        suffix = suffix.astype(jnp.bfloat16).astype(jnp.float32)
        scores_grad = jnp.where(causal[None], jnp.einsum('bti,bsi->bts', grad_wide, value_wide), 0.0)
        scores_grad = scores_grad.astype(jnp.bfloat16).astype(jnp.float32)
        scores = jnp.where(causal[None], jnp.einsum('bti,bsi->bts', query_wide, key_wide), 0.0)
        scores = scores.astype(jnp.bfloat16).astype(jnp.float32)
        grad_query = jnp.einsum('bts,bsi->bti', scores_grad, key_wide) + jnp.einsum('btj,bij->bti', grad_wide, prefix)
        grad_key = jnp.einsum('bts,bti->bsi', scores_grad, query_wide) + jnp.einsum('bsj,bij->bsi', value_wide, suffix)
        grad_value = jnp.einsum('bts,btj->bsj', scores, grad_wide) + jnp.einsum('bsi,bij->bsj', key_wide, suffix)
        outputs = []
        for result in (grad_query, grad_key, grad_value):
            outputs.append((factor * result).astype(jnp.bfloat16).reshape(SEQ, DH))
        return (outputs[0], outputs[1], outputs[2])
    stacked = lax.map(one_head, jnp.arange(H, dtype=jnp.int32))
    finals = []
    for result in stacked:
        finals.append(jnp.transpose(result, (1, 0, 2)).reshape(SEQ, H * DH))
    return (finals[0], finals[1], finals[2])
```

```python
import math

import jax
import jax.numpy as jnp
from jax import lax
from jax.experimental import pallas as pl
from jax.experimental.pallas import tpu as pltpu
from jax.sharding import PartitionSpec as P

DH = 128
NY = 4
ZG = 4
F32 = jnp.float32
BF16 = jnp.bfloat16


def groups(ctx):
    nz = ctx // NY
    y_line = [[z * NY + y for y in range(NY)] for z in range(nz)]
    z_line = [[z * NY + y for z in range(nz)] for y in range(NY)]
    z_near = [[(g * ZG + i) * NY + y for i in range(ZG)] for g in range(nz // ZG) for y in range(NY)]
    z_far = [[(g * ZG + i) * NY + y for g in range(nz // ZG)] for i in range(ZG) for y in range(NY)]
    return y_line, z_line, z_near, z_far


def exchange(pieces, group):
    return lax.all_to_all(pieces, "ctx", 0, 0, axis_index_groups=group)


def call(kernel, out_shape, flops, size, smem=()):
    def run(*operands):
        specs = [
            pl.BlockSpec(memory_space=pltpu.SMEM if i in smem else pltpu.VMEM) for i in range(len(operands))
        ]
        many = isinstance(out_shape, (list, tuple))
        out_specs = [pl.BlockSpec(memory_space=pltpu.VMEM)] * len(out_shape) if many else pl.BlockSpec(memory_space=pltpu.VMEM)
        return pl.pallas_call(
            kernel,
            out_shape=out_shape,
            in_specs=specs,
            out_specs=out_specs,
            compiler_params=pltpu.CompilerParams(vmem_limit_bytes=40 * 1024 * 1024),
            cost_estimate=pl.CostEstimate(flops=flops, bytes_accessed=size, transcendentals=0),
        )(*operands)

    return run


def shape(dims, dtype=BF16):
    return jax.ShapeDtypeStruct(dims, dtype)


def dot(a, b, ca, cb):
    return lax.dot_general(a, b, (((ca,), (cb,)), ((), ())), preferred_element_type=F32)


def pack_kernel(q_ref, k_ref, v_ref, g_ref, out_ref):
    for y in range(NY):
        for at, ref in enumerate((q_ref, k_ref, v_ref)):
            out_ref[y, at] = ref[:, y * DH : (y + 1) * DH]
        rows = g_ref.shape[1] // (2 * NY)
        low = g_ref[:, y * rows : (y + 1) * rows]
        high = g_ref[:, (NY + y) * rows : (NY + y + 1) * rows]
        out_ref[y, 3] = jnp.concatenate([low, high], axis=1)


def product_kernel(a_ref, b_ref, out_ref):
    tokens = a_ref.shape[0]
    step = tokens // NY
    for t in range(NY):
        rows = pl.ds(t * step, step)
        part = dot(a_ref[rows, :], b_ref[...], 1, 0).astype(BF16)
        for h in range(NY):
            out_ref[h, rows, :] = part[:, h * DH : (h + 1) * DH]


def state_kernel(packed_ref, part_ref, grad_ref, states_ref, copies_ref):
    step = packed_ref.shape[2]
    total_k = jnp.zeros((DH, DH), F32)
    total_q = jnp.zeros((DH, DH), F32)
    for b in range(NY):
        rows = pl.ds(b * step, step)
        grad = part_ref[0, rows, :].astype(F32)
        for y in range(1, NY):
            grad = grad + part_ref[y, rows, :].astype(F32)
        grad = grad.astype(BF16)
        grad_ref[rows, :] = grad
        key_state = dot(packed_ref[b, 1], packed_ref[b, 2], 0, 0)
        query_state = dot(packed_ref[b, 0], grad, 0, 0)
        states_ref[0, b] = key_state
        states_ref[1, b] = query_state
        total_k = total_k + key_state
        total_q = total_q + query_state
    for i in range(ZG):
        copies_ref[i, 0] = total_k.astype(BF16)
        copies_ref[i, 1] = total_q.astype(BF16)


def final_kernel(factor, place_ref, packed_ref, grad_ref, states_ref, near_ref, far_ref, out_ref):
    step = packed_ref.shape[2]
    inner, outer = place_ref[0], place_ref[1]
    prefix = jnp.zeros((DH, DH), F32)
    suffix = jnp.zeros((DH, DH), F32)
    for i in range(near_ref.shape[0]):
        prefix = prefix + jnp.where(i < inner, near_ref[i, 0].astype(F32), 0.0)
        suffix = suffix + jnp.where(i > inner, near_ref[i, 1].astype(F32), 0.0)
    for i in range(far_ref.shape[0]):
        other = far_ref[i].astype(F32)
        prefix = prefix + jnp.where(i < outer, other, 0.0)
        suffix = suffix + jnp.where(i > outer, other, 0.0)
    suffixes = [suffix]
    for b in range(NY - 1, 0, -1):
        suffix = suffix + states_ref[1, b]
        suffixes.append(suffix)
    suffixes = suffixes[::-1]
    row = lax.broadcasted_iota(jnp.int32, (step, step), 0)
    col = lax.broadcasted_iota(jnp.int32, (step, step), 1)
    lower = row >= col
    upper = row <= col
    for b in range(NY):
        query, key, value = packed_ref[b, 0], packed_ref[b, 1], packed_ref[b, 2]
        grad = grad_ref[b * step : (b + 1) * step, :]
        before = prefix.astype(BF16)
        after = suffixes[b].astype(BF16)
        scores_grad = jnp.where(lower, dot(grad, value, 1, 1), 0.0).astype(BF16)
        scores_grad_t = jnp.where(upper, dot(value, grad, 1, 1), 0.0).astype(BF16)
        scores_t = jnp.where(upper, dot(key, query, 1, 1), 0.0).astype(BF16)
        grad_q = dot(scores_grad, key, 1, 0) + dot(grad, before, 1, 1)
        grad_k = dot(scores_grad_t, query, 1, 0) + dot(value, after, 1, 1)
        grad_v = dot(scores_t, grad, 1, 0) + dot(key, after, 1, 0)
        out_ref[b, 0] = (factor * grad_q).astype(BF16)
        out_ref[b, 1] = (factor * grad_k).astype(BF16)
        out_ref[b, 2] = (factor * grad_v).astype(BF16)
        prefix = prefix + states_ref[0, b]


def unpack_kernel(in_ref, q_ref, k_ref, v_ref):
    for h in range(NY):
        for at, ref in enumerate((q_ref, k_ref, v_ref)):
            ref[:, h * DH : (h + 1) * DH] = in_ref[h, at]


def local(queries, keys, values, grad_out, out_weight):
    step, width = queries.shape
    ctx, tp = lax.axis_size("ctx"), lax.axis_size("tp")
    nz = ctx // NY
    tokens = NY * step
    depth = nz * out_weight.shape[0]
    factor = 1.0 / math.sqrt(step * ctx)
    y_line, z_line, z_near, z_far = groups(ctx)
    z = lax.axis_index("ctx") // NY
    place = jnp.stack([z % ZG, z // ZG]).astype(jnp.int32)

    packed = call(pack_kernel, shape((NY, 4, step, DH)), 0, 8 * step * width * 2)(queries, keys, values, grad_out)
    packed = exchange(packed, y_line)
    mine = packed[:, 3].reshape(tokens, DH)
    full_grad = lax.all_gather(mine, "tp", axis=1, tiled=True)
    weight = exchange(jnp.broadcast_to(out_weight[None], (nz,) + out_weight.shape), z_line)
    weight = weight.reshape(depth, width)
    parts = call(product_kernel, shape((NY, tokens, DH)), 2 * tokens * depth * width, 4 * 1024 * 1024)(full_grad, weight)
    parts = exchange(parts, y_line)
    grads, states, copies = call(
        state_kernel,
        [shape((tokens, DH)), shape((2, NY, DH, DH), F32), shape((ZG, 2, DH, DH))],
        4 * tokens * DH * DH,
        3 * 1024 * 1024,
    )(packed, parts)
    near = exchange(copies, z_near)
    total = jnp.sum(near.astype(F32), axis=0).astype(BF16)
    other = jnp.arange(nz // ZG, dtype=jnp.int32)[:, None, None]
    far = exchange(jnp.where(other < place[1], total[1][None], total[0][None]), z_far)
    result = call(
        lambda *refs: final_kernel(factor, *refs),
        shape((NY, 3, step, DH)),
        8 * 2 * tokens * step * DH,
        3 * 1024 * 1024,
        smem=(0,),
    )(place, packed, grads, states, near, far)
    result = exchange(result, y_line)
    out = shape((step, width))
    return tuple(call(unpack_kernel, [out, out, out], 0, 6 * step * width * 2)(result))


def solution(mesh):
    placed = P("ctx", "tp")
    return jax.shard_map(
        local,
        mesh=mesh,
        in_specs=(placed,) * 5,
        out_specs=(placed,) * 3,
        check_vma=False,
    )
```

```python
import math

import jax
import jax.numpy as jnp
from jax import lax
from jax.experimental import pallas as pl
from jax.experimental.pallas import tpu as pltpu
from jax.sharding import PartitionSpec as P

DH = 128
NY = 4
ZG = 4
F32 = jnp.float32
BF16 = jnp.bfloat16


def groups(ctx):
    nz = ctx // NY
    y_line = [[z * NY + y for y in range(NY)] for z in range(nz)]
    z_line = [[z * NY + y for z in range(nz)] for y in range(NY)]
    z_near = [[(g * ZG + i) * NY + y for i in range(ZG)] for g in range(nz // ZG) for y in range(NY)]
    z_far = [[(g * ZG + i) * NY + y for g in range(nz // ZG)] for i in range(ZG) for y in range(NY)]
    return y_line, z_line, z_near, z_far


def exchange(pieces, group):
    return lax.all_to_all(pieces, "ctx", 0, 0, axis_index_groups=group)


def call(kernel, out_shape, flops, size, smem=(), hbm=(), scratch=(), out_hbm=False):
    def run(*operands):
        specs = [
            pl.BlockSpec(memory_space=pltpu.SMEM if i in smem else pltpu.HBM if i in hbm else pltpu.VMEM)
            for i in range(len(operands))
        ]
        operands = [
            pltpu.with_memory_space_constraint(x, pltpu.HBM) if i in hbm else x for i, x in enumerate(operands)
        ]
        many = isinstance(out_shape, (list, tuple))
        out_specs = [pl.BlockSpec(memory_space=pltpu.VMEM)] * len(out_shape) if many else pl.BlockSpec(memory_space=pltpu.HBM if out_hbm else pltpu.VMEM)
        return pl.pallas_call(
            kernel,
            out_shape=out_shape,
            in_specs=specs,
            out_specs=out_specs,
            scratch_shapes=scratch,
            compiler_params=pltpu.CompilerParams(vmem_limit_bytes=40 * 1024 * 1024),
            cost_estimate=pl.CostEstimate(flops=flops, bytes_accessed=size, transcendentals=0),
        )(*operands)

    return run


def shape(dims, dtype=BF16):
    return jax.ShapeDtypeStruct(dims, dtype)


def dot(a, b, ca, cb):
    return lax.dot_general(a, b, (((ca,), (cb,)), ((), ())), preferred_element_type=F32)


def pack_kernel(q_ref, k_ref, v_ref, g_ref, out_ref, grad, sems):
    load = pltpu.make_async_copy(g_ref, grad, sems.at[NY, 0])
    load.start()
    moves = []
    for y in range(NY):
        for at, ref in enumerate((q_ref, k_ref, v_ref)):
            move = pltpu.make_async_copy(ref.at[:, pl.ds(y * DH, DH)], out_ref.at[y, at], sems.at[y, at])
            move.start()
            moves.append(move)
    load.wait()
    rows = grad.shape[1] // (2 * NY)
    for y in range(NY):
        low = grad[:, y * rows : (y + 1) * rows]
        high = grad[:, (NY + y) * rows : (NY + y + 1) * rows]
        out_ref[y, 3] = jnp.concatenate([low, high], axis=1)
    for move in moves:
        move.wait()


def product_kernel(place_ref, a0_ref, a1_ref, a2_ref, a3_ref, b_ref, out_ref):
    tokens, depth = a0_ref.shape
    step = tokens // NY
    held = (a0_ref, a1_ref, a2_ref, a3_ref)
    chips = len(held)
    for t in range(NY):
        rows = pl.ds(t * step, step)
        part = jnp.zeros((step, b_ref.shape[1]), F32)
        for d, ref in enumerate(held):
            chip = lax.rem(place_ref[2] + (chips - d), chips)
            start = pl.multiple_of(chip * depth, depth)
            part = part + dot(ref[rows, :], b_ref[pl.ds(start, depth), :], 1, 0)
        part = part.astype(BF16)
        for h in range(NY):
            out_ref[h, rows, :] = part[:, h * DH : (h + 1) * DH]


def state_kernel(packed_ref, part_ref, grad_ref, states_ref, copies_ref):
    step = packed_ref.shape[2]
    total_k = jnp.zeros((DH, DH), F32)
    total_q = jnp.zeros((DH, DH), F32)
    for b in range(NY):
        rows = pl.ds(b * step, step)
        grad = part_ref[0, rows, :].astype(F32)
        for y in range(1, NY):
            grad = grad + part_ref[y, rows, :].astype(F32)
        grad = grad.astype(BF16)
        grad_ref[rows, :] = grad
        key_state = dot(packed_ref[b, 1], packed_ref[b, 2], 0, 0)
        query_state = dot(packed_ref[b, 0], grad, 0, 0)
        states_ref[0, b] = key_state
        states_ref[1, b] = query_state
        total_k = total_k + key_state
        total_q = total_q + query_state
    for i in range(ZG):
        copies_ref[i, 0] = total_k.astype(BF16)
        copies_ref[i, 1] = total_q.astype(BF16)


def final_kernel(factor, place_ref, packed_ref, grad_ref, states_ref, near_ref, far_ref, out_ref):
    step = packed_ref.shape[2]
    inner, outer = place_ref[0], place_ref[1]
    prefix = jnp.zeros((DH, DH), F32)
    suffix = jnp.zeros((DH, DH), F32)
    for i in range(near_ref.shape[0]):
        prefix = prefix + jnp.where(i < inner, near_ref[i, 0].astype(F32), 0.0)
        suffix = suffix + jnp.where(i > inner, near_ref[i, 1].astype(F32), 0.0)
    for i in range(far_ref.shape[0]):
        other = far_ref[i].astype(F32)
        prefix = prefix + jnp.where(i < outer, other, 0.0)
        suffix = suffix + jnp.where(i > outer, other, 0.0)
    suffixes = [suffix]
    for b in range(NY - 1, 0, -1):
        suffix = suffix + states_ref[1, b]
        suffixes.append(suffix)
    suffixes = suffixes[::-1]
    row = lax.broadcasted_iota(jnp.int32, (step, step), 0)
    col = lax.broadcasted_iota(jnp.int32, (step, step), 1)
    lower = row >= col
    upper = row <= col
    for b in range(NY):
        query, key, value = packed_ref[b, 0], packed_ref[b, 1], packed_ref[b, 2]
        grad = grad_ref[b * step : (b + 1) * step, :]
        before = prefix.astype(BF16)
        after = suffixes[b].astype(BF16)
        scores_grad = jnp.where(lower, dot(grad, value, 1, 1), 0.0).astype(BF16)
        scores_grad_t = jnp.where(upper, dot(value, grad, 1, 1), 0.0).astype(BF16)
        scores_t = jnp.where(upper, dot(key, query, 1, 1), 0.0).astype(BF16)
        grad_q = dot(scores_grad, key, 1, 0) + dot(grad, before, 1, 1)
        grad_k = dot(scores_grad_t, query, 1, 0) + dot(value, after, 1, 1)
        grad_v = dot(scores_t, grad, 1, 0) + dot(key, after, 1, 0)
        out_ref[b, 0] = (factor * grad_q).astype(BF16)
        out_ref[b, 1] = (factor * grad_k).astype(BF16)
        out_ref[b, 2] = (factor * grad_v).astype(BF16)
        prefix = prefix + states_ref[0, b]


def unpack_kernel(in_ref, q_ref, k_ref, v_ref):
    for h in range(NY):
        for at, ref in enumerate((q_ref, k_ref, v_ref)):
            ref[:, h * DH : (h + 1) * DH] = in_ref[h, at]


def local(queries, keys, values, grad_out, out_weight):
    step, width = queries.shape
    ctx, tp = lax.axis_size("ctx"), lax.axis_size("tp")
    nz = ctx // NY
    tokens = NY * step
    depth = nz * out_weight.shape[0]
    factor = 1.0 / math.sqrt(step * ctx)
    y_line, z_line, z_near, z_far = groups(ctx)
    at = lax.axis_index("tp")
    z = lax.axis_index("ctx") // NY
    place = jnp.stack([z % ZG, z // ZG, at // 2]).astype(jnp.int32)
    earlier = jnp.arange(nz // ZG, dtype=jnp.int32) < place[1]
    first = at % 2 == 0
    queries, place, earlier, first = lax.optimization_barrier((queries, place, earlier, first))

    packed = call(
        pack_kernel,
        shape((NY, 4, step, DH)),
        0,
        8 * step * width * 2,
        hbm=range(4),
        scratch=[pltpu.VMEM((step, width), BF16), pltpu.SemaphoreType.DMA((NY + 1, 3))],
    )(queries, keys, values, grad_out)
    packed = exchange(packed, y_line)
    mine = packed[:, 3].reshape(tokens, DH)
    swap = [(t, t ^ 1) for t in range(tp)]
    other = lax.ppermute(mine, "tp", swap)
    pair = jnp.concatenate([jnp.where(first, mine, other), jnp.where(first, other, mine)], axis=1)
    shares = [pair]
    for d in range(1, tp // 2):
        shares.append(lax.ppermute(pair, "tp", [(t, (t + 2 * d) % tp) for t in range(tp)]))
    shard = out_weight.shape[0]
    main = shard - shard // 8
    rest, pair_seen = lax.optimization_barrier((out_weight, pair))
    weight = lax.all_gather(rest[:main], "ctx", axis_index_groups=z_line)
    last = exchange(jnp.broadcast_to(rest[None, main:], (nz, shard - main, width)), z_line)
    weight = jnp.concatenate([weight, last], axis=1).reshape(depth, width)
    parts = call(
        product_kernel,
        shape((NY, tokens, DH)),
        2 * tokens * depth * width,
        4 * 1024 * 1024,
        smem=(0,),
    )(place, *shares, weight)
    parts = exchange(parts, y_line)
    grads, states, copies = call(
        state_kernel,
        [shape((tokens, DH)), shape((2, NY, DH, DH), F32), shape((ZG, 2, DH, DH))],
        4 * tokens * DH * DH,
        3 * 1024 * 1024,
    )(packed, parts)
    near = exchange(copies, z_near)
    total = jnp.sum(near.astype(F32), axis=0).astype(BF16)
    far = exchange(jnp.where(earlier[:, None, None], total[1][None], total[0][None]), z_far)
    result = call(
        lambda *refs: final_kernel(factor, *refs),
        shape((NY, 3, step, DH)),
        8 * 2 * tokens * step * DH,
        3 * 1024 * 1024,
        smem=(0,),
    )(place, packed, grads, states, near, far)
    result = exchange(result, y_line)
    out = shape((step, width))
    return tuple(call(unpack_kernel, [out, out, out], 0, 6 * step * width * 2)(result))


def solution(mesh):
    placed = P("ctx", "tp")
    return jax.shard_map(
        local,
        mesh=mesh,
        in_specs=(placed,) * 5,
        out_specs=(placed,) * 3,
        check_vma=False,
    )
```

```python
import math

import jax
import jax.numpy as jnp
from jax import lax
from jax.experimental import pallas as pl
from jax.experimental.pallas import tpu as pltpu
from jax.sharding import PartitionSpec as P

DH = 128
NY = 4
ZG = 4
F32 = jnp.float32
BF16 = jnp.bfloat16


def groups(ctx):
    nz = ctx // NY
    y_line = [[z * NY + y for y in range(NY)] for z in range(nz)]
    z_line = [[z * NY + y for z in range(nz)] for y in range(NY)]
    z_near = [[(g * ZG + i) * NY + y for i in range(ZG)] for g in range(nz // ZG) for y in range(NY)]
    z_far = [[(g * ZG + i) * NY + y for g in range(nz // ZG)] for i in range(ZG) for y in range(NY)]
    return y_line, z_line, z_near, z_far


def exchange(pieces, group):
    return lax.all_to_all(pieces, "ctx", 0, 0, axis_index_groups=group)


def call(kernel, out_shape, flops, size, smem=(), hbm=(), scratch=(), out_hbm=False):
    def run(*operands):
        specs = [
            pl.BlockSpec(memory_space=pltpu.SMEM if i in smem else pltpu.HBM if i in hbm else pltpu.VMEM)
            for i in range(len(operands))
        ]
        operands = [
            pltpu.with_memory_space_constraint(x, pltpu.HBM) if i in hbm else x for i, x in enumerate(operands)
        ]
        many = isinstance(out_shape, (list, tuple))
        out_specs = [pl.BlockSpec(memory_space=pltpu.VMEM)] * len(out_shape) if many else pl.BlockSpec(memory_space=pltpu.HBM if out_hbm else pltpu.VMEM)
        return pl.pallas_call(
            kernel,
            out_shape=out_shape,
            in_specs=specs,
            out_specs=out_specs,
            scratch_shapes=scratch,
            compiler_params=pltpu.CompilerParams(vmem_limit_bytes=40 * 1024 * 1024),
            cost_estimate=pl.CostEstimate(flops=flops, bytes_accessed=size, transcendentals=0),
        )(*operands)

    return run


def shape(dims, dtype=BF16):
    return jax.ShapeDtypeStruct(dims, dtype)


def dot(a, b, ca, cb):
    return lax.dot_general(a, b, (((ca,), (cb,)), ((), ())), preferred_element_type=F32)


def block_of(place_ref, d):
    return lax.rem(place_ref[2] + (NY - d), NY)


def pack_kernel(place_ref, q_ref, k_ref, v_ref, g_ref, *rest):
    outs, (grad, pieces, sems) = rest[:NY], rest[NY:]
    load = pltpu.make_async_copy(g_ref, grad, sems.at[NY, 0])
    load.start()
    moves = []
    for d, out_ref in enumerate(outs):
        start = pl.multiple_of(lax.rem(place_ref[2] + d, NY) * DH, DH)
        for at, ref in enumerate((q_ref, k_ref, v_ref)):
            move = pltpu.make_async_copy(ref.at[:, pl.ds(start, DH)], out_ref.at[at], sems.at[d, at])
            move.start()
            moves.append(move)
    load.wait()
    rows = grad.shape[1] // (2 * NY)
    for y in range(NY):
        low = grad[:, y * rows : (y + 1) * rows]
        high = grad[:, (NY + y) * rows : (NY + y + 1) * rows]
        pieces[y] = jnp.concatenate([low, high], axis=1)
    for d, out_ref in enumerate(outs):
        out_ref[3] = pieces[lax.rem(place_ref[2] + d, NY)]
    for move in moves:
        move.wait()


def mine_kernel(*refs):
    step = refs[0].shape[1]
    for d in range(NY):
        refs[NY][d * step : (d + 1) * step, :] = refs[d][3]


def pair_kernel(place_ref, mine_ref, other_ref, out_ref):
    first = place_ref[4] == 0
    mine, other = mine_ref[...], other_ref[...]
    out_ref[:, :DH] = jnp.where(first, mine, other)
    out_ref[:, DH:] = jnp.where(first, other, mine)


def product_kernel(place_ref, a0_ref, a1_ref, a2_ref, a3_ref, main_ref, last_ref, out_ref, weight):
    tokens, depth = a0_ref.shape
    step = tokens // NY
    held = (a0_ref, a1_ref, a2_ref, a3_ref)
    chips = len(held)
    main, last = main_ref.shape[1], last_ref.shape[1]
    for z in range(main_ref.shape[0]):
        low = z * (main + last)
        weight[low : low + main, :] = main_ref[z]
        weight[low + main : low + main + last, :] = last_ref[z]
    for t in range(NY):
        part = jnp.zeros((step, weight.shape[1]), F32)
        for d, ref in enumerate(held):
            chip = lax.rem(place_ref[3] + (chips - d), chips)
            start = pl.multiple_of(chip * depth, depth)
            part = part + dot(ref[t * step : (t + 1) * step, :], weight[pl.ds(start, depth), :], 1, 0)
        part = part.astype(BF16)
        rows = pl.ds(pl.multiple_of(block_of(place_ref, t) * step, step), step)
        for h in range(NY):
            out_ref[h, rows, :] = part[:, h * DH : (h + 1) * DH]


def state_kernel(place_ref, p0_ref, p1_ref, p2_ref, p3_ref, part_ref, grad_ref, states_ref, copies_ref):
    step = p0_ref.shape[1]
    total_k = jnp.zeros((DH, DH), F32)
    total_q = jnp.zeros((DH, DH), F32)
    for d, ref in enumerate((p0_ref, p1_ref, p2_ref, p3_ref)):
        rows = pl.ds(pl.multiple_of(block_of(place_ref, d) * step, step), step)
        grad = part_ref[0, rows, :].astype(F32)
        for y in range(1, NY):
            grad = grad + part_ref[y, rows, :].astype(F32)
        grad = grad.astype(BF16)
        grad_ref[d] = grad
        key_state = dot(ref[1], ref[2], 0, 0)
        query_state = dot(ref[0], grad, 0, 0)
        states_ref[0, d] = key_state
        states_ref[1, d] = query_state
        total_k = total_k + key_state
        total_q = total_q + query_state
    for i in range(ZG):
        copies_ref[i, 0] = total_k.astype(BF16)
        copies_ref[i, 1] = total_q.astype(BF16)


def final_kernel(factor, place_ref, p0_ref, p1_ref, p2_ref, p3_ref, grad_ref, states_ref, near_ref, far_ref, out_ref):
    step = p0_ref.shape[1]
    inner, outer = place_ref[0], place_ref[1]
    prefix = jnp.zeros((DH, DH), F32)
    suffix = jnp.zeros((DH, DH), F32)
    for i in range(near_ref.shape[0]):
        prefix = prefix + jnp.where(i < inner, near_ref[i, 0].astype(F32), 0.0)
        suffix = suffix + jnp.where(i > inner, near_ref[i, 1].astype(F32), 0.0)
    for i in range(far_ref.shape[0]):
        other = far_ref[i].astype(F32)
        prefix = prefix + jnp.where(i < outer, other, 0.0)
        suffix = suffix + jnp.where(i > outer, other, 0.0)
    row = lax.broadcasted_iota(jnp.int32, (step, step), 0)
    col = lax.broadcasted_iota(jnp.int32, (step, step), 1)
    lower = row >= col
    upper = row <= col
    for d, ref in enumerate((p0_ref, p1_ref, p2_ref, p3_ref)):
        block = block_of(place_ref, d)
        query, key, value = ref[0], ref[1], ref[2]
        grad = grad_ref[d]
        before, after = prefix, suffix
        for e in range(NY):
            if e != d:
                other = block_of(place_ref, e)
                before = before + jnp.where(other < block, states_ref[0, e], 0.0)
                after = after + jnp.where(other > block, states_ref[1, e], 0.0)
        before = before.astype(BF16)
        after = after.astype(BF16)
        scores_grad = jnp.where(lower, dot(grad, value, 1, 1), 0.0).astype(BF16)
        scores_grad_t = jnp.where(upper, dot(value, grad, 1, 1), 0.0).astype(BF16)
        scores_t = jnp.where(upper, dot(key, query, 1, 1), 0.0).astype(BF16)
        grad_q = dot(scores_grad, key, 1, 0) + dot(grad, before, 1, 1)
        grad_k = dot(scores_grad_t, query, 1, 0) + dot(value, after, 1, 1)
        grad_v = dot(scores_t, grad, 1, 0) + dot(key, after, 1, 0)
        out_ref[block, 0] = (factor * grad_q).astype(BF16)
        out_ref[block, 1] = (factor * grad_k).astype(BF16)
        out_ref[block, 2] = (factor * grad_v).astype(BF16)


def unpack_kernel(in_ref, q_ref, k_ref, v_ref):
    for h in range(NY):
        for at, ref in enumerate((q_ref, k_ref, v_ref)):
            ref[:, h * DH : (h + 1) * DH] = in_ref[h, at]


def local(queries, keys, values, grad_out, out_weight):
    step, width = queries.shape
    ctx, tp = lax.axis_size("ctx"), lax.axis_size("tp")
    nz = ctx // NY
    tokens = NY * step
    depth = nz * out_weight.shape[0]
    factor = 1.0 / math.sqrt(step * ctx)
    y_line, z_line, z_near, z_far = groups(ctx)
    at = lax.axis_index("tp")
    here = lax.axis_index("ctx")
    z = here // NY
    place = jnp.stack([z % ZG, z // ZG, here % NY, at // 2, at % 2]).astype(jnp.int32)
    earlier = jnp.arange(nz // ZG, dtype=jnp.int32) < place[1]
    queries, place, earlier = lax.optimization_barrier((queries, place, earlier))

    packed = call(
        pack_kernel,
        [shape((4, step, DH))] * NY,
        0,
        8 * step * width * 2,
        smem=(0,),
        hbm=range(1, 5),
        scratch=[
            pltpu.VMEM((step, width), BF16),
            pltpu.VMEM((NY, step, DH), BF16),
            pltpu.SemaphoreType.DMA((NY + 1, 3)),
        ],
    )(place, queries, keys, values, grad_out)
    packed = list(packed)
    for d in (1, 3, 2):
        turn = [(i, i // NY * NY + (i + d) % NY) for i in range(ctx)]
        packed[d] = lax.ppermute(packed[d], "ctx", turn)
    mine = call(mine_kernel, shape((tokens, DH)), 0, 4 * tokens * DH)(*packed)
    other = lax.ppermute(mine, "tp", [(t, t ^ 1) for t in range(tp)])
    pair = call(pair_kernel, shape((tokens, 2 * DH)), 0, 8 * tokens * DH, smem=(0,))(place, mine, other)
    shares = [pair]
    for d in range(1, tp // 2):
        shares.append(lax.ppermute(pair, "tp", [(t, (t + 2 * d) % tp) for t in range(tp)]))
    shard = out_weight.shape[0]
    main = shard - shard // 4
    kept, pair_seen = lax.optimization_barrier((out_weight, pair))
    weight = lax.all_gather(kept[:main], "ctx", axis_index_groups=z_line)
    last = exchange(jnp.broadcast_to(out_weight[None, main:], (nz, shard - main, width)), z_line)
    parts = call(
        product_kernel,
        shape((NY, tokens, DH)),
        2 * tokens * depth * width,
        4 * 1024 * 1024,
        smem=(0,),
        scratch=[pltpu.VMEM((depth, width), BF16)],
    )(place, *shares, weight, last)
    parts = exchange(parts, y_line)
    grads, states, copies = call(
        state_kernel,
        [shape((NY, step, DH)), shape((2, NY, DH, DH), F32), shape((ZG, 2, DH, DH))],
        4 * tokens * DH * DH,
        3 * 1024 * 1024,
        smem=(0,),
    )(place, *packed, parts)
    near = exchange(copies, z_near)
    total = jnp.sum(near.astype(F32), axis=0).astype(BF16)
    far = exchange(jnp.where(earlier[:, None, None], total[1][None], total[0][None]), z_far)
    result = call(
        lambda *refs: final_kernel(factor, *refs),
        shape((NY, 3, step, DH)),
        8 * 2 * tokens * step * DH,
        3 * 1024 * 1024,
        smem=(0,),
    )(place, *packed, grads, states, near, far)
    result = exchange(result, y_line)
    out = shape((step, width))
    return tuple(call(unpack_kernel, [out, out, out], 0, 6 * step * width * 2)(result))


def solution(mesh):
    placed = P("ctx", "tp")
    return jax.shard_map(
        local,
        mesh=mesh,
        in_specs=(placed,) * 5,
        out_specs=(placed,) * 3,
        check_vma=False,
    )
```

```python
import math

import jax
import jax.numpy as jnp
from jax import lax
from jax.experimental import pallas as pl
from jax.experimental.pallas import tpu as pltpu
from jax.sharding import PartitionSpec as P

DH = 128
NY = 4
NX = 4
ZG = 4
F32 = jnp.float32
BF16 = jnp.bfloat16


def groups(ctx):
    nz = ctx // NY
    y_line = [[z * NY + y for y in range(NY)] for z in range(nz)]
    z_line = [[z * NY + y for z in range(nz)] for y in range(NY)]
    z_near = [[(g * ZG + i) * NY + y for i in range(ZG)] for g in range(nz // ZG) for y in range(NY)]
    z_far = [[(g * ZG + i) * NY + y for g in range(nz // ZG)] for i in range(ZG) for y in range(NY)]
    return y_line, z_line, z_near, z_far


def exchange(pieces, group):
    return lax.all_to_all(pieces, "ctx", 0, 0, axis_index_groups=group)


def call(kernel, out_shape, flops, size, smem=(), hbm=(), anywhere=(), scratch=(), out_hbm=False):
    def run(*operands):
        specs = [
            pl.BlockSpec(memory_space=pltpu.SMEM if i in smem else pltpu.HBM if i in hbm else pl.ANY if i in anywhere else pltpu.VMEM)
            for i in range(len(operands))
        ]
        operands = [
            pltpu.with_memory_space_constraint(x, pltpu.HBM) if i in hbm else x for i, x in enumerate(operands)
        ]
        many = isinstance(out_shape, (list, tuple))
        out_specs = [pl.BlockSpec(memory_space=pltpu.VMEM)] * len(out_shape) if many else pl.BlockSpec(memory_space=pltpu.HBM if out_hbm else pltpu.VMEM)
        return pl.pallas_call(
            kernel,
            out_shape=out_shape,
            in_specs=specs,
            out_specs=out_specs,
            scratch_shapes=scratch,
            compiler_params=pltpu.CompilerParams(vmem_limit_bytes=16 * 1024 * 1024),
            cost_estimate=pl.CostEstimate(flops=flops, bytes_accessed=size, transcendentals=0),
        )(*operands)

    return run


def shape(dims, dtype=BF16):
    return jax.ShapeDtypeStruct(dims, dtype)


def dot(a, b, ca, cb):
    return lax.dot_general(a, b, (((ca,), (cb,)), ((), ())), preferred_element_type=F32)


def block_of(place_ref, d):
    return lax.rem(place_ref[2] + (NY - d), NY)


def pack_kernel(place_ref, q_ref, k_ref, v_ref, g_ref, *rest):
    outs, (grad, pieces, sems) = rest[:NY], rest[NY:]
    load = pltpu.make_async_copy(g_ref, grad, sems.at[NY, 0])
    load.start()
    moves = []
    for d, out_ref in enumerate(outs):
        start = pl.multiple_of(lax.rem(place_ref[2] + d, NY) * DH, DH)
        for at, ref in enumerate((q_ref, k_ref, v_ref)):
            move = pltpu.make_async_copy(ref.at[:, pl.ds(start, DH)], out_ref.at[at], sems.at[d, at])
            move.start()
            moves.append(move)
    load.wait()
    rows = grad.shape[1] // (2 * NY)
    for y in range(NY):
        low = grad[:, y * rows : (y + 1) * rows]
        high = grad[:, (NY + y) * rows : (NY + y + 1) * rows]
        pieces[y] = jnp.concatenate([low, high], axis=1)
    for d, out_ref in enumerate(outs):
        out_ref[3] = pieces[lax.rem(place_ref[2] + d, NY)]
    for move in moves:
        move.wait()


def mine_kernel(*refs):
    step = refs[0].shape[1]
    for d in range(NY):
        refs[NY][d * step : (d + 1) * step, :] = refs[d][3]


def copies_kernel(w_ref, out_ref, held, sem, sems):
    load = pltpu.make_async_copy(w_ref, held, sem)
    load.start()
    load.wait()
    moves = []
    for z in range(out_ref.shape[0]):
        move = pltpu.make_async_copy(held, out_ref.at[z], sems.at[z])
        move.start()
        moves.append(move)
    for move in moves:
        move.wait()


def product_kernel(place_ref, *refs):
    weight, early_ref, out_ref, held, sems = refs[2 * NX :]
    tokens, depth = refs[0].shape
    step = tokens // NY
    core = place_ref[4]
    loads = []
    for t in range(NY):
        tile = pl.ds(t * step, step)
        for i in range(2 * NX):
            lanes = pl.ds(i // NX * depth, depth)
            load = pltpu.make_async_copy(refs[i].at[tile, :], held.at[i % NX, tile, lanes], sems.at[t, i])
            load.start()
            loads.append(load)
    for t in range(NY):
        part = jnp.zeros((step, weight.shape[1]), F32)
        for load in loads[t * 2 * NX : (t + 1) * 2 * NX]:
            load.wait()
        for d in range(NX):
            chip = lax.rem(place_ref[3] + (NX - d), NX)
            own = pl.multiple_of((chip * 2 + core) * depth, depth)
            far = pl.multiple_of((chip * 2 + 1 - core) * depth, depth)
            rows = jnp.concatenate([weight[pl.ds(own, depth), :], weight[pl.ds(far, depth), :]], axis=0)
            part = part + dot(held[d, t * step : (t + 1) * step, :], rows, 1, 0)
        part = part.astype(BF16)
        rows = pl.ds(pl.multiple_of(block_of(place_ref, t) * step, step), step)
        for h in range(NY):
            out_ref[h, rows, :] = part[:, h * DH : (h + 1) * DH]


def key_kernel(p0_ref, p1_ref, p2_ref, p3_ref, states_ref, scores_ref):
    step = p0_ref.shape[1]
    row = lax.broadcasted_iota(jnp.int32, (step, step), 0)
    col = lax.broadcasted_iota(jnp.int32, (step, step), 1)
    for d, ref in enumerate((p0_ref, p1_ref, p2_ref, p3_ref)):
        states_ref[d] = dot(ref[1], ref[2], 0, 0)
        scores_ref[d] = jnp.where(row <= col, dot(ref[1], ref[0], 1, 1), 0.0).astype(BF16)


def state_kernel(place_ref, p0_ref, p1_ref, p2_ref, p3_ref, part_ref, key_ref, grad_ref, query_ref, copies_ref):
    step = p0_ref.shape[1]
    total_k = jnp.zeros((DH, DH), F32)
    total_q = jnp.zeros((DH, DH), F32)
    for d, ref in enumerate((p0_ref, p1_ref, p2_ref, p3_ref)):
        rows = pl.ds(pl.multiple_of(block_of(place_ref, d) * step, step), step)
        grad = part_ref[0, rows, :].astype(F32)
        for y in range(1, NY):
            grad = grad + part_ref[y, rows, :].astype(F32)
        grad = grad.astype(BF16)
        grad_ref[d] = grad
        query_state = dot(ref[0], grad, 0, 0)
        query_ref[d] = query_state
        total_k = total_k + key_ref[d]
        total_q = total_q + query_state
    for i in range(ZG):
        copies_ref[i, 0] = total_k.astype(BF16)
        copies_ref[i, 1] = total_q.astype(BF16)


def final_kernel(factor, place_ref, p0_ref, p1_ref, p2_ref, p3_ref, grad_ref, key_ref, query_ref, scores_ref, near_ref, far_ref, out_ref):
    step = p0_ref.shape[1]
    inner, outer = place_ref[0], place_ref[1]
    prefix = jnp.zeros((DH, DH), F32)
    suffix = jnp.zeros((DH, DH), F32)
    for i in range(near_ref.shape[0]):
        prefix = prefix + jnp.where(i < inner, near_ref[i, 0].astype(F32), 0.0)
        suffix = suffix + jnp.where(i > inner, near_ref[i, 1].astype(F32), 0.0)
    for i in range(far_ref.shape[0]):
        other = far_ref[i].astype(F32)
        prefix = prefix + jnp.where(i < outer, other, 0.0)
        suffix = suffix + jnp.where(i > outer, other, 0.0)
    row = lax.broadcasted_iota(jnp.int32, (step, step), 0)
    col = lax.broadcasted_iota(jnp.int32, (step, step), 1)
    lower = row >= col
    upper = row <= col
    for d, ref in enumerate((p0_ref, p1_ref, p2_ref, p3_ref)):
        block = block_of(place_ref, d)
        query, key, value = ref[0], ref[1], ref[2]
        grad = grad_ref[d]
        before, after = prefix, suffix
        for e in range(NY):
            if e != d:
                other = block_of(place_ref, e)
                before = before + jnp.where(other < block, key_ref[e], 0.0)
                after = after + jnp.where(other > block, query_ref[e], 0.0)
        before = before.astype(BF16)
        after = after.astype(BF16)
        scores_grad = jnp.where(lower, dot(grad, value, 1, 1), 0.0).astype(BF16)
        scores_grad_t = jnp.where(upper, dot(value, grad, 1, 1), 0.0).astype(BF16)
        scores_t = scores_ref[d]
        grad_q = dot(scores_grad, key, 1, 0) + dot(grad, before, 1, 1)
        grad_k = dot(scores_grad_t, query, 1, 0) + dot(value, after, 1, 1)
        grad_v = dot(scores_t, grad, 1, 0) + dot(key, after, 1, 0)
        out_ref[block, 0] = (factor * grad_q).astype(BF16)
        out_ref[block, 1] = (factor * grad_k).astype(BF16)
        out_ref[block, 2] = (factor * grad_v).astype(BF16)


def unpack_kernel(in_ref, q_ref, k_ref, v_ref):
    for h in range(NY):
        for at, ref in enumerate((q_ref, k_ref, v_ref)):
            ref[:, h * DH : (h + 1) * DH] = in_ref[h, at]


def local(queries, keys, values, grad_out, out_weight):
    step, width = queries.shape
    ctx, tp = lax.axis_size("ctx"), lax.axis_size("tp")
    nz = ctx // NY
    tokens = NY * step
    depth = nz * out_weight.shape[0]
    factor = 1.0 / math.sqrt(step * ctx)
    y_line, z_line, z_near, z_far = groups(ctx)
    at = lax.axis_index("tp")
    here = lax.axis_index("ctx")
    z = here // NY
    place = jnp.stack([z % ZG, z // ZG, here % NY, at // 2, at % 2]).astype(jnp.int32)
    earlier = jnp.arange(nz // ZG, dtype=jnp.int32) < place[1]
    grad_out, place, earlier = lax.optimization_barrier((grad_out, place, earlier))

    copies = call(
        copies_kernel,
        pltpu.HBM((nz,) + out_weight.shape, BF16),
        0,
        2 * depth * width,
        hbm=(0,),
        out_hbm=True,
        scratch=[pltpu.VMEM(out_weight.shape, BF16), pltpu.SemaphoreType.DMA, pltpu.SemaphoreType.DMA((nz,))],
    )(out_weight)
    weight = exchange(copies, z_line).reshape(depth, width)
    grad_out, copies = lax.optimization_barrier((grad_out, copies))
    turns = {d: [(i, i // NY * NY + (i + d) % NY) for i in range(ctx)] for d in (1, 3, 2)}
    packed = call(
        pack_kernel,
        [shape((4, step, DH))] * NY,
        0,
        8 * step * width * 2,
        smem=(0,),
        hbm=range(1, 5),
        scratch=[
            pltpu.VMEM((step, width), BF16),
            pltpu.VMEM((NY, step, DH), BF16),
            pltpu.SemaphoreType.DMA((NY + 1, 3)),
        ],
    )(place, queries, keys, values, grad_out)
    packed = list(packed)
    for d, turn in turns.items():
        packed[d] = lax.ppermute(packed[d], "ctx", turn)
    mine = call(mine_kernel, shape((tokens, DH)), 0, 4 * tokens * DH)(*packed)
    shares = [mine]
    for d in range(1, NX):
        shares.append(lax.ppermute(mine, "tp", [(t, (t + 2 * d) % tp) for t in range(tp)]))
    swap = [(t, t ^ 1) for t in range(tp)]
    shares = shares + [lax.ppermute(share, "tp", swap) for share in shares]
    key_states, scores = call(
        key_kernel,
        [shape((NY, DH, DH), F32), shape((NY, step, step))],
        4 * tokens * DH * (DH + step),
        2 * 1024 * 1024,
    )(*packed)
    parts = call(
        product_kernel,
        shape((NY, tokens, DH)),
        2 * tokens * depth * width,
        4 * 1024 * 1024,
        smem=(0,),
        hbm=range(1, 2 * NX + 1),
        anywhere=(2 * NX + 2,),
        scratch=[pltpu.VMEM((NX, tokens, 2 * DH), BF16), pltpu.SemaphoreType.DMA((NY, 2 * NX))],
    )(place, *shares, weight, scores)
    parts = exchange(parts, y_line)
    grads, query_states, copies = call(
        state_kernel,
        [shape((NY, step, DH)), shape((NY, DH, DH), F32), shape((ZG, 2, DH, DH))],
        4 * tokens * DH * DH,
        3 * 1024 * 1024,
        smem=(0,),
    )(place, *packed, parts, key_states)
    near = exchange(copies, z_near)
    total = jnp.sum(near.astype(F32), axis=0).astype(BF16)
    far = exchange(jnp.where(earlier[:, None, None], total[1][None], total[0][None]), z_far)
    result = call(
        lambda *refs: final_kernel(factor, *refs),
        shape((NY, 3, step, DH)),
        8 * 2 * tokens * step * DH,
        3 * 1024 * 1024,
        smem=(0,),
    )(place, *packed, grads, key_states, query_states, scores, near, far)
    result = exchange(result, y_line)
    out = shape((step, width))
    return tuple(call(unpack_kernel, [out, out, out], 0, 6 * step * width * 2)(result))


def solution(mesh):
    placed = P("ctx", "tp")
    return jax.shard_map(
        local,
        mesh=mesh,
        in_specs=(placed,) * 5,
        out_specs=(placed,) * 3,
        check_vma=False,
    )
```

```python
import math

import jax
import jax.numpy as jnp
from jax import lax
from jax.experimental import pallas as pl
from jax.experimental.pallas import tpu as pltpu
from jax.sharding import PartitionSpec as P

DH = 128
NY = 4
NX = 4
ZG = 4
LINE = (2, 1, 3, 0)
NEAR = (2, 1, 3, 0)
FAR = (2, 1, 3, 0)
F32 = jnp.float32
BF16 = jnp.bfloat16


def groups(ctx):
    nz = ctx // NY
    y_line = [[z * NY + y for y in LINE] for z in range(nz)]
    z_line = [[z * NY + y for z in range(nz)] for y in range(NY)]
    z_near = [[(g * ZG + i) * NY + y for i in NEAR] for g in range(nz // ZG) for y in range(NY)]
    z_far = [[(g * ZG + i) * NY + y for g in FAR] for i in range(ZG) for y in range(NY)]
    return y_line, z_line, z_near, z_far


def exchange(pieces, group):
    return lax.all_to_all(pieces, "ctx", 0, 0, axis_index_groups=group)


def call(kernel, out_shape, flops, size, smem=(), hbm=(), anywhere=(), scratch=(), out_hbm=False):
    def run(*operands):
        specs = [
            pl.BlockSpec(memory_space=pltpu.SMEM if i in smem else pltpu.HBM if i in hbm else pl.ANY if i in anywhere else pltpu.VMEM)
            for i in range(len(operands))
        ]
        operands = [
            pltpu.with_memory_space_constraint(x, pltpu.HBM) if i in hbm else x for i, x in enumerate(operands)
        ]
        many = isinstance(out_shape, (list, tuple))
        out_specs = [pl.BlockSpec(memory_space=pltpu.VMEM)] * len(out_shape) if many else pl.BlockSpec(memory_space=pltpu.HBM if out_hbm else pltpu.VMEM)
        return pl.pallas_call(
            kernel,
            out_shape=out_shape,
            in_specs=specs,
            out_specs=out_specs,
            scratch_shapes=scratch,
            compiler_params=pltpu.CompilerParams(vmem_limit_bytes=16 * 1024 * 1024),
            cost_estimate=pl.CostEstimate(flops=flops, bytes_accessed=size, transcendentals=0),
        )(*operands)

    return run


def shape(dims, dtype=BF16):
    return jax.ShapeDtypeStruct(dims, dtype)


def dot(a, b, ca, cb):
    return lax.dot_general(a, b, (((ca,), (cb,)), ((), ())), preferred_element_type=F32)


def block_of(place_ref, d):
    return lax.rem(place_ref[2] + (NY - d), NY)


def pack_kernel(place_ref, q_ref, k_ref, v_ref, g_ref, *rest):
    outs, (grad, pieces, sems) = rest[:NY], rest[NY:]
    load = pltpu.make_async_copy(g_ref, grad, sems.at[NY, 0])
    load.start()
    moves = []
    for d, out_ref in enumerate(outs):
        start = pl.multiple_of(lax.rem(place_ref[2] + d, NY) * DH, DH)
        for at, ref in enumerate((q_ref, k_ref, v_ref)):
            move = pltpu.make_async_copy(ref.at[:, pl.ds(start, DH)], out_ref.at[at], sems.at[d, at])
            move.start()
            moves.append(move)
    load.wait()
    rows = grad.shape[1] // (2 * NY)
    for y in range(NY):
        low = grad[:, y * rows : (y + 1) * rows]
        high = grad[:, (NY + y) * rows : (NY + y + 1) * rows]
        pieces[y] = jnp.concatenate([low, high], axis=1)
    for d, out_ref in enumerate(outs):
        out_ref[3] = pieces[lax.rem(place_ref[2] + d, NY)]
    for move in moves:
        move.wait()


def mine_kernel(*refs):
    step = refs[0].shape[1]
    for d in range(NY):
        refs[NY][d * step : (d + 1) * step, :] = refs[d][3]


def copies_kernel(w_ref, out_ref, held, sem, sems):
    load = pltpu.make_async_copy(w_ref, held, sem)
    load.start()
    load.wait()
    moves = []
    for z in range(out_ref.shape[0]):
        move = pltpu.make_async_copy(held, out_ref.at[z], sems.at[z])
        move.start()
        moves.append(move)
    for move in moves:
        move.wait()


def product_kernel(place_ref, *refs):
    weight, early_ref, out_ref, held, sems = refs[2 * NX :]
    tokens, depth = refs[0].shape
    step = tokens // NY
    core = place_ref[4]
    loads = []
    for t in range(NY):
        tile = pl.ds(t * step, step)
        for i in range(2 * NX):
            lanes = pl.ds(i // NX * depth, depth)
            loads.append(pltpu.make_async_copy(refs[i].at[tile, :], held.at[i % NX, tile, lanes], sems.at[t, i]))
    for load in loads:
        load.start()
    for t in range(NY):
        part = jnp.zeros((step, weight.shape[1]), F32)
        for load in loads[t * 2 * NX : (t + 1) * 2 * NX]:
            load.wait()
        for d in range(NX):
            chip = lax.rem(place_ref[3] + (NX - d), NX)
            own = pl.multiple_of((chip * 2 + core) * depth, depth)
            far = pl.multiple_of((chip * 2 + 1 - core) * depth, depth)
            rows = jnp.concatenate([weight[pl.ds(own, depth), :], weight[pl.ds(far, depth), :]], axis=0)
            part = part + dot(held[d, t * step : (t + 1) * step, :], rows, 1, 0)
        part = part.astype(BF16)
        rows = pl.ds(pl.multiple_of(block_of(place_ref, t) * step, step), step)
        for i, h in enumerate(LINE):
            out_ref[i, rows, :] = part[:, h * DH : (h + 1) * DH]


def key_kernel(p0_ref, p1_ref, p2_ref, p3_ref, states_ref, scores_ref):
    step = p0_ref.shape[1]
    row = lax.broadcasted_iota(jnp.int32, (step, step), 0)
    col = lax.broadcasted_iota(jnp.int32, (step, step), 1)
    for d, ref in enumerate((p0_ref, p1_ref, p2_ref, p3_ref)):
        states_ref[d] = dot(ref[1], ref[2], 0, 0)
        scores_ref[d] = jnp.where(row <= col, dot(ref[1], ref[0], 1, 1), 0.0).astype(BF16)


def state_kernel(place_ref, p0_ref, p1_ref, p2_ref, p3_ref, part_ref, key_ref, grad_ref, query_ref, copies_ref):
    step = p0_ref.shape[1]
    total_k = jnp.zeros((DH, DH), F32)
    total_q = jnp.zeros((DH, DH), F32)
    for d, ref in enumerate((p0_ref, p1_ref, p2_ref, p3_ref)):
        rows = pl.ds(pl.multiple_of(block_of(place_ref, d) * step, step), step)
        grad = part_ref[0, rows, :].astype(F32)
        for y in range(1, NY):
            grad = grad + part_ref[y, rows, :].astype(F32)
        grad = grad.astype(BF16)
        grad_ref[d] = grad
        query_state = dot(ref[0], grad, 0, 0)
        query_ref[d] = query_state
        total_k = total_k + key_ref[d]
        total_q = total_q + query_state
    for i in range(ZG):
        copies_ref[i, 0] = total_k.astype(BF16)
        copies_ref[i, 1] = total_q.astype(BF16)


def final_kernel(factor, place_ref, p0_ref, p1_ref, p2_ref, p3_ref, grad_ref, key_ref, query_ref, scores_ref, near_ref, far_ref, out_ref):
    step = p0_ref.shape[1]
    inner, outer = place_ref[0], place_ref[1]
    prefix = jnp.zeros((DH, DH), F32)
    suffix = jnp.zeros((DH, DH), F32)
    for i in range(near_ref.shape[0]):
        prefix = prefix + jnp.where(NEAR[i] < inner, near_ref[i, 0].astype(F32), 0.0)
        suffix = suffix + jnp.where(NEAR[i] > inner, near_ref[i, 1].astype(F32), 0.0)
    for i in range(far_ref.shape[0]):
        other = far_ref[i].astype(F32)
        prefix = prefix + jnp.where(FAR[i] < outer, other, 0.0)
        suffix = suffix + jnp.where(FAR[i] > outer, other, 0.0)
    row = lax.broadcasted_iota(jnp.int32, (step, step), 0)
    col = lax.broadcasted_iota(jnp.int32, (step, step), 1)
    lower = row >= col
    upper = row <= col
    for d, ref in enumerate((p0_ref, p1_ref, p2_ref, p3_ref)):
        block = block_of(place_ref, d)
        query, key, value = ref[0], ref[1], ref[2]
        grad = grad_ref[d]
        before, after = prefix, suffix
        for e in range(NY):
            if e != d:
                other = block_of(place_ref, e)
                before = before + jnp.where(other < block, key_ref[e], 0.0)
                after = after + jnp.where(other > block, query_ref[e], 0.0)
        before = before.astype(BF16)
        after = after.astype(BF16)
        scores_grad = jnp.where(lower, dot(grad, value, 1, 1), 0.0).astype(BF16)
        scores_grad_t = jnp.where(upper, dot(value, grad, 1, 1), 0.0).astype(BF16)
        scores_t = scores_ref[d]
        grad_q = dot(scores_grad, key, 1, 0) + dot(grad, before, 1, 1)
        grad_k = dot(scores_grad_t, query, 1, 0) + dot(value, after, 1, 1)
        grad_v = dot(scores_t, grad, 1, 0) + dot(key, after, 1, 0)
        to = sum(jnp.where(block == h, i, 0) for i, h in enumerate(LINE))
        out_ref[to, 0] = (factor * grad_q).astype(BF16)
        out_ref[to, 1] = (factor * grad_k).astype(BF16)
        out_ref[to, 2] = (factor * grad_v).astype(BF16)


def unpack_kernel(in_ref, q_ref, k_ref, v_ref):
    for i, h in enumerate(LINE):
        for at, ref in enumerate((q_ref, k_ref, v_ref)):
            ref[:, h * DH : (h + 1) * DH] = in_ref[i, at]


def local(queries, keys, values, grad_out, out_weight):
    step, width = queries.shape
    ctx, tp = lax.axis_size("ctx"), lax.axis_size("tp")
    nz = ctx // NY
    tokens = NY * step
    depth = nz * out_weight.shape[0]
    factor = 1.0 / math.sqrt(step * ctx)
    y_line, z_line, z_near, z_far = groups(ctx)
    at = lax.axis_index("tp")
    here = lax.axis_index("ctx")
    z = here // NY
    place = jnp.stack([z % ZG, z // ZG, here % NY, at // 2, at % 2]).astype(jnp.int32)
    earlier = jnp.array(FAR, jnp.int32) < place[1]
    grad_out, place, earlier = lax.optimization_barrier((grad_out, place, earlier))

    copies = call(
        copies_kernel,
        pltpu.HBM((nz,) + out_weight.shape, BF16),
        0,
        2 * depth * width,
        hbm=(0,),
        out_hbm=True,
        scratch=[pltpu.VMEM(out_weight.shape, BF16), pltpu.SemaphoreType.DMA, pltpu.SemaphoreType.DMA((nz,))],
    )(out_weight)
    weight = exchange(copies, z_line).reshape(depth, width)
    grad_out, copies = lax.optimization_barrier((grad_out, copies))
    turns = {d: [(i, i // NY * NY + (i + d) % NY) for i in range(ctx)] for d in (1, 3, 2)}
    packed = call(
        pack_kernel,
        [shape((4, step, DH))] * NY,
        0,
        8 * step * width * 2,
        smem=(0,),
        hbm=range(1, 5),
        scratch=[
            pltpu.VMEM((step, width), BF16),
            pltpu.VMEM((NY, step, DH), BF16),
            pltpu.SemaphoreType.DMA((NY + 1, 3)),
        ],
    )(place, queries, keys, values, grad_out)
    packed = list(packed)
    for d, turn in turns.items():
        packed[d] = lax.ppermute(packed[d], "ctx", turn)
    mine = call(mine_kernel, shape((tokens, DH)), 0, 4 * tokens * DH)(*packed)
    shares = [mine]
    for d in range(1, NX):
        shares.append(lax.ppermute(mine, "tp", [(t, (t + 2 * d) % tp) for t in range(tp)]))
    swap = [(t, t ^ 1) for t in range(tp)]
    shares = shares + [lax.ppermute(share, "tp", swap) for share in shares]
    key_states, scores = call(
        key_kernel,
        [shape((NY, DH, DH), F32), shape((NY, step, step))],
        4 * tokens * DH * (DH + step),
        2 * 1024 * 1024,
    )(*packed)
    parts = call(
        product_kernel,
        shape((NY, tokens, DH)),
        2 * tokens * depth * width,
        4 * 1024 * 1024,
        smem=(0,),
        hbm=range(1, 2 * NX + 1),
        anywhere=(2 * NX + 2,),
        scratch=[pltpu.VMEM((NX, tokens, 2 * DH), BF16), pltpu.SemaphoreType.DMA((NY, 2 * NX))],
    )(place, *shares, weight, scores)
    parts = exchange(parts, y_line)
    grads, query_states, copies = call(
        state_kernel,
        [shape((NY, step, DH)), shape((NY, DH, DH), F32), shape((ZG, 2, DH, DH))],
        4 * tokens * DH * DH,
        3 * 1024 * 1024,
        smem=(0,),
    )(place, *packed, parts, key_states)
    near = exchange(copies, z_near)
    total = jnp.sum(near.astype(F32), axis=0).astype(BF16)
    far = exchange(jnp.where(earlier[:, None, None], total[1][None], total[0][None]), z_far)
    result = call(
        lambda *refs: final_kernel(factor, *refs),
        shape((NY, 3, step, DH)),
        8 * 2 * tokens * step * DH,
        3 * 1024 * 1024,
        smem=(0,),
    )(place, *packed, grads, key_states, query_states, scores, near, far)
    result = exchange(result, y_line)
    out = shape((step, width))
    return tuple(call(unpack_kernel, [out, out, out], 0, 6 * step * width * 2)(result))


def solution(mesh):
    placed = P("ctx", "tp")
    return jax.shard_map(
        local,
        mesh=mesh,
        in_specs=(placed,) * 5,
        out_specs=(placed,) * 3,
        check_vma=False,
    )
```

```python
import math

import jax
import jax.numpy as jnp
from jax import lax
from jax.experimental import pallas as pl
from jax.experimental.pallas import tpu as pltpu
from jax.sharding import PartitionSpec as P

DH = 128
NY = 4
NX = 4
ZG = 4
LINE = (2, 1, 3, 0)
NEAR = (2, 1, 3, 0)
FAR = (2, 1, 3, 0)
F32 = jnp.float32
BF16 = jnp.bfloat16


def groups(ctx):
    nz = ctx // NY
    y_line = [[z * NY + y for y in LINE] for z in range(nz)]
    z_line = [[z * NY + y for z in range(nz)] for y in range(NY)]
    z_near = [[(g * ZG + i) * NY + y for i in NEAR] for g in range(nz // ZG) for y in range(NY)]
    z_far = [[(g * ZG + i) * NY + y for g in FAR] for i in range(ZG) for y in range(NY)]
    return y_line, z_line, z_near, z_far


def exchange(pieces, group):
    return lax.all_to_all(pieces, "ctx", 0, 0, axis_index_groups=group)


def call(kernel, out_shape, flops, size, smem=(), hbm=(), anywhere=(), scratch=(), out_hbm=False):
    def run(*operands):
        specs = [
            pl.BlockSpec(memory_space=pltpu.SMEM if i in smem else pltpu.HBM if i in hbm else pl.ANY if i in anywhere else pltpu.VMEM)
            for i in range(len(operands))
        ]
        operands = [
            pltpu.with_memory_space_constraint(x, pltpu.HBM) if i in hbm else x for i, x in enumerate(operands)
        ]
        many = isinstance(out_shape, (list, tuple))
        out_specs = [pl.BlockSpec(memory_space=pltpu.VMEM)] * len(out_shape) if many else pl.BlockSpec(memory_space=pltpu.HBM if out_hbm else pltpu.VMEM)
        return pl.pallas_call(
            kernel,
            out_shape=out_shape,
            in_specs=specs,
            out_specs=out_specs,
            scratch_shapes=scratch,
            compiler_params=pltpu.CompilerParams(vmem_limit_bytes=16 * 1024 * 1024),
            cost_estimate=pl.CostEstimate(flops=flops, bytes_accessed=size, transcendentals=0),
        )(*operands)

    return run


def shape(dims, dtype=BF16):
    return jax.ShapeDtypeStruct(dims, dtype)


def dot(a, b, ca, cb):
    return lax.dot_general(a, b, (((ca,), (cb,)), ((), ())), preferred_element_type=F32)


def block_of(place_ref, d):
    return lax.rem(place_ref[2] + (NY - d), NY)


def pack_kernel(place_ref, q_ref, k_ref, v_ref, g_ref, *rest):
    outs, (grad, pieces, sems) = rest[:NY], rest[NY:]
    load = pltpu.make_async_copy(g_ref, grad, sems.at[NY, 0])
    load.start()
    moves = []
    for d, out_ref in enumerate(outs):
        start = pl.multiple_of(lax.rem(place_ref[2] + d, NY) * DH, DH)
        for at, ref in enumerate((q_ref, k_ref, v_ref)):
            move = pltpu.make_async_copy(ref.at[:, pl.ds(start, DH)], out_ref.at[at], sems.at[d, at])
            move.start()
            moves.append(move)
    load.wait()
    rows = grad.shape[1] // (2 * NY)
    for y in range(NY):
        low = grad[:, y * rows : (y + 1) * rows]
        high = grad[:, (NY + y) * rows : (NY + y + 1) * rows]
        pieces[y] = jnp.concatenate([low, high], axis=1)
    for d, out_ref in enumerate(outs):
        out_ref[3] = pieces[lax.rem(place_ref[2] + d, NY)]
    for move in moves:
        move.wait()


def mine_kernel(*refs):
    step = refs[0].shape[1]
    for d in range(NY):
        refs[NY][d * step : (d + 1) * step, :] = refs[d][3]


def copies_kernel(w_ref, out_ref, held, sem, sems):
    load = pltpu.make_async_copy(w_ref, held, sem)
    load.start()
    load.wait()
    moves = []
    for z in range(out_ref.shape[0]):
        move = pltpu.make_async_copy(held, out_ref.at[z], sems.at[z])
        move.start()
        moves.append(move)
    for move in moves:
        move.wait()


def product_kernel(place_ref, *refs):
    weight_ref, early_ref, out_ref, weight, sems = refs[2 * NX :]
    tokens, depth = refs[0].shape
    step = tokens // NY
    core = place_ref[4]
    loads = []
    for d in range(NX):
        chip = lax.rem(place_ref[3] + (NX - d), NX)
        start = pl.multiple_of(chip * 2 * depth, 2 * depth)
        load = pltpu.make_async_copy(weight_ref.at[pl.ds(start, 2 * depth), :], weight.at[d], sems.at[d])
        load.start()
        loads.append(load)
    own = pl.multiple_of(core * depth, depth)
    far = pl.multiple_of((1 - core) * depth, depth)
    for t in range(NY):
        part = jnp.zeros((step, weight.shape[2]), F32)
        tile = slice(t * step, (t + 1) * step)
        for d in range(NX):
            if t == 0:
                loads[d].wait()
            held = jnp.concatenate([refs[d][tile, :], refs[NX + d][tile, :]], axis=1)
            rows = jnp.concatenate([weight[d, pl.ds(own, depth), :], weight[d, pl.ds(far, depth), :]], axis=0)
            part = part + dot(held, rows, 1, 0)
        part = part.astype(BF16)
        rows = pl.ds(pl.multiple_of(block_of(place_ref, t) * step, step), step)
        for i, h in enumerate(LINE):
            out_ref[i, rows, :] = part[:, h * DH : (h + 1) * DH]


def key_kernel(p0_ref, p1_ref, p2_ref, p3_ref, states_ref):
    for d, ref in enumerate((p0_ref, p1_ref, p2_ref, p3_ref)):
        states_ref[d] = dot(ref[1], ref[2], 0, 0)


def state_kernel(place_ref, p0_ref, p1_ref, p2_ref, p3_ref, part_ref, key_ref, grad_ref, query_ref, copies_ref):
    step = p0_ref.shape[1]
    total_k = jnp.zeros((DH, DH), F32)
    total_q = jnp.zeros((DH, DH), F32)
    for d, ref in enumerate((p0_ref, p1_ref, p2_ref, p3_ref)):
        rows = pl.ds(pl.multiple_of(block_of(place_ref, d) * step, step), step)
        grad = part_ref[0, rows, :].astype(F32)
        for y in range(1, NY):
            grad = grad + part_ref[y, rows, :].astype(F32)
        grad = grad.astype(BF16)
        grad_ref[d] = grad
        query_state = dot(ref[0], grad, 0, 0)
        query_ref[d] = query_state
        total_k = total_k + key_ref[d]
        total_q = total_q + query_state
    for i in range(ZG):
        copies_ref[i, 0] = total_k.astype(BF16)
        copies_ref[i, 1] = total_q.astype(BF16)


def final_kernel(factor, place_ref, p0_ref, p1_ref, p2_ref, p3_ref, grad_ref, key_ref, query_ref, near_ref, far_ref, out_ref):
    step = p0_ref.shape[1]
    inner, outer = place_ref[0], place_ref[1]
    prefix = jnp.zeros((DH, DH), F32)
    suffix = jnp.zeros((DH, DH), F32)
    for i in range(near_ref.shape[0]):
        prefix = prefix + jnp.where(NEAR[i] < inner, near_ref[i, 0].astype(F32), 0.0)
        suffix = suffix + jnp.where(NEAR[i] > inner, near_ref[i, 1].astype(F32), 0.0)
    for i in range(far_ref.shape[0]):
        other = far_ref[i].astype(F32)
        prefix = prefix + jnp.where(FAR[i] < outer, other, 0.0)
        suffix = suffix + jnp.where(FAR[i] > outer, other, 0.0)
    row = lax.broadcasted_iota(jnp.int32, (step, step), 0)
    col = lax.broadcasted_iota(jnp.int32, (step, step), 1)
    lower = row >= col
    upper = row <= col
    for d, ref in enumerate((p0_ref, p1_ref, p2_ref, p3_ref)):
        block = block_of(place_ref, d)
        query, key, value = ref[0], ref[1], ref[2]
        grad = grad_ref[d]
        before, after = prefix, suffix
        for e in range(NY):
            if e != d:
                other = block_of(place_ref, e)
                before = before + jnp.where(other < block, key_ref[e], 0.0)
                after = after + jnp.where(other > block, query_ref[e], 0.0)
        before = before.astype(BF16)
        after = after.astype(BF16)
        scores_grad = jnp.where(lower, dot(grad, value, 1, 1), 0.0).astype(BF16)
        scores_grad_t = jnp.where(upper, dot(value, grad, 1, 1), 0.0).astype(BF16)
        scores_t = jnp.where(upper, dot(key, query, 1, 1), 0.0).astype(BF16)
        grad_q = dot(scores_grad, key, 1, 0) + dot(grad, before, 1, 1)
        grad_k = dot(scores_grad_t, query, 1, 0) + dot(value, after, 1, 1)
        grad_v = dot(scores_t, grad, 1, 0) + dot(key, after, 1, 0)
        to = sum(jnp.where(block == h, i, 0) for i, h in enumerate(LINE))
        out_ref[to, 0] = (factor * grad_q).astype(BF16)
        out_ref[to, 1] = (factor * grad_k).astype(BF16)
        out_ref[to, 2] = (factor * grad_v).astype(BF16)


def unpack_kernel(in_ref, q_ref, k_ref, v_ref):
    for i, h in enumerate(LINE):
        for at, ref in enumerate((q_ref, k_ref, v_ref)):
            ref[:, h * DH : (h + 1) * DH] = in_ref[i, at]


def local(queries, keys, values, grad_out, out_weight):
    step, width = queries.shape
    ctx, tp = lax.axis_size("ctx"), lax.axis_size("tp")
    nz = ctx // NY
    tokens = NY * step
    depth = nz * out_weight.shape[0]
    factor = 1.0 / math.sqrt(step * ctx)
    y_line, z_line, z_near, z_far = groups(ctx)
    at = lax.axis_index("tp")
    here = lax.axis_index("ctx")
    z = here // NY
    place = jnp.stack([z % ZG, z // ZG, here % NY, at // 2, at % 2]).astype(jnp.int32)
    slot = jnp.arange(nz // ZG, dtype=jnp.int32)
    earlier = sum(jnp.where(slot == i, g, 0) for i, g in enumerate(FAR)) < place[1]
    grad_out, place, earlier = lax.optimization_barrier((grad_out, place, earlier))

    copies = call(
        copies_kernel,
        pltpu.HBM((nz,) + out_weight.shape, BF16),
        0,
        2 * depth * width,
        hbm=(0,),
        out_hbm=True,
        scratch=[pltpu.VMEM(out_weight.shape, BF16), pltpu.SemaphoreType.DMA, pltpu.SemaphoreType.DMA((nz,))],
    )(out_weight)
    weight = exchange(copies, z_line).reshape(depth, width)
    grad_out, copies = lax.optimization_barrier((grad_out, copies))
    turns = {d: [(i, i // NY * NY + (i + d) % NY) for i in range(ctx)] for d in (1, 3, 2)}
    packed = call(
        pack_kernel,
        [shape((4, step, DH))] * NY,
        0,
        8 * step * width * 2,
        smem=(0,),
        hbm=range(1, 5),
        scratch=[
            pltpu.VMEM((step, width), BF16),
            pltpu.VMEM((NY, step, DH), BF16),
            pltpu.SemaphoreType.DMA((NY + 1, 3)),
        ],
    )(place, queries, keys, values, grad_out)
    packed = list(packed)
    for d, turn in turns.items():
        packed[d] = lax.ppermute(packed[d], "ctx", turn)
    mine = call(mine_kernel, shape((tokens, DH)), 0, 4 * tokens * DH)(*packed)
    shares = [mine]
    for d in range(1, NX):
        shares.append(lax.ppermute(mine, "tp", [(t, (t + 2 * d) % tp) for t in range(tp)]))
    swap = [(t, t ^ 1) for t in range(tp)]
    shares = shares + [lax.ppermute(share, "tp", swap) for share in shares]
    key_states = call(
        key_kernel,
        shape((NY, DH, DH), F32),
        4 * tokens * DH * (DH + step),
        2 * 1024 * 1024,
    )(*packed)
    parts = call(
        product_kernel,
        shape((NY, tokens, DH)),
        2 * tokens * depth * width,
        4 * 1024 * 1024,
        smem=(0,),
        hbm=(2 * NX + 1,),
        anywhere=(2 * NX + 2,),
        scratch=[pltpu.VMEM((NX, depth // NX, width), BF16), pltpu.SemaphoreType.DMA((NX,))],
    )(place, *shares, weight, key_states)
    parts = exchange(parts, y_line)
    grads, query_states, copies = call(
        state_kernel,
        [shape((NY, step, DH)), shape((NY, DH, DH), F32), shape((ZG, 2, DH, DH))],
        4 * tokens * DH * DH,
        3 * 1024 * 1024,
        smem=(0,),
    )(place, *packed, parts, key_states)
    near = exchange(copies, z_near)
    total = jnp.sum(near.astype(F32), axis=0).astype(BF16)
    far = exchange(jnp.where(earlier[:, None, None], total[1][None], total[0][None]), z_far)
    result = call(
        lambda *refs: final_kernel(factor, *refs),
        shape((NY, 3, step, DH)),
        8 * 2 * tokens * step * DH,
        3 * 1024 * 1024,
        smem=(0,),
    )(place, *packed, grads, key_states, query_states, near, far)
    result = exchange(result, y_line)
    out = shape((step, width))
    return tuple(call(unpack_kernel, [out, out, out], 0, 6 * step * width * 2)(result))


def solution(mesh):
    placed = P("ctx", "tp")
    return jax.shard_map(
        local,
        mesh=mesh,
        in_specs=(placed,) * 5,
        out_specs=(placed,) * 3,
        check_vma=False,
    )
```

```python
import math

import jax
import jax.numpy as jnp
from jax import lax
from jax.experimental import pallas as pl
from jax.experimental.pallas import tpu as pltpu
from jax.sharding import PartitionSpec as P

DH = 128
NY = 4
NX = 4
ZG = 4
LINE = (2, 1, 3, 0)
NEAR = (2, 1, 3, 0)
FAR = (2, 1, 3, 0)
F32 = jnp.float32
BF16 = jnp.bfloat16


def groups(ctx):
    nz = ctx // NY
    y_line = [[z * NY + y for y in LINE] for z in range(nz)]
    z_line = [[z * NY + y for z in range(p, nz, 2)] for p in range(2) for y in range(NY)]
    z_near = [[(g * ZG + i) * NY + y for i in NEAR] for g in range(nz // ZG) for y in range(NY)]
    z_far = [[(g * ZG + i) * NY + y for g in FAR] for i in range(ZG) for y in range(NY)]
    return y_line, z_line, z_near, z_far


def exchange(pieces, group):
    return lax.all_to_all(pieces, "ctx", 0, 0, axis_index_groups=group)


def call(kernel, out_shape, flops, size, smem=(), hbm=(), anywhere=(), scratch=(), out_hbm=False):
    def run(*operands):
        specs = [
            pl.BlockSpec(memory_space=pltpu.SMEM if i in smem else pltpu.HBM if i in hbm else pl.ANY if i in anywhere else pltpu.VMEM)
            for i in range(len(operands))
        ]
        operands = [
            pltpu.with_memory_space_constraint(x, pltpu.HBM) if i in hbm else x for i, x in enumerate(operands)
        ]
        many = isinstance(out_shape, (list, tuple))
        out_specs = [pl.BlockSpec(memory_space=pltpu.VMEM)] * len(out_shape) if many else pl.BlockSpec(memory_space=pltpu.HBM if out_hbm else pltpu.VMEM)
        return pl.pallas_call(
            kernel,
            out_shape=out_shape,
            in_specs=specs,
            out_specs=out_specs,
            scratch_shapes=scratch,
            compiler_params=pltpu.CompilerParams(vmem_limit_bytes=16 * 1024 * 1024),
            cost_estimate=pl.CostEstimate(flops=flops, bytes_accessed=size, transcendentals=0),
        )(*operands)

    return run


def shape(dims, dtype=BF16):
    return jax.ShapeDtypeStruct(dims, dtype)


def dot(a, b, ca, cb):
    return lax.dot_general(a, b, (((ca,), (cb,)), ((), ())), preferred_element_type=F32)


def block_of(place_ref, d):
    return lax.rem(place_ref[2] + (NY - d), NY)


def pack_kernel(place_ref, q_ref, k_ref, v_ref, g_ref, *rest):
    outs, (grad, pieces, sems) = rest[:NY], rest[NY:]
    load = pltpu.make_async_copy(g_ref, grad, sems.at[NY, 0])
    load.start()
    moves = []
    for d, out_ref in enumerate(outs):
        start = pl.multiple_of(lax.rem(place_ref[2] + d, NY) * DH, DH)
        for at, ref in enumerate((q_ref, k_ref, v_ref)):
            move = pltpu.make_async_copy(ref.at[:, pl.ds(start, DH)], out_ref.at[at], sems.at[d, at])
            move.start()
            moves.append(move)
    load.wait()
    rows = grad.shape[1] // (2 * NY)
    for y in range(NY):
        low = grad[:, y * rows : (y + 1) * rows]
        high = grad[:, (NY + y) * rows : (NY + y + 1) * rows]
        pieces[y] = jnp.concatenate([low, high], axis=1)
    for d, out_ref in enumerate(outs):
        out_ref[3] = pieces[lax.rem(place_ref[2] + d, NY)]
    for move in moves:
        move.wait()


def mine_kernel(*refs):
    step = refs[0].shape[1]
    for d in range(NY):
        refs[NY][d * step : (d + 1) * step, :] = refs[d][3]


def copies_kernel(w_ref, out_ref, held, sem, sems):
    load = pltpu.make_async_copy(w_ref, held, sem)
    load.start()
    load.wait()
    moves = []
    for z in range(out_ref.shape[0]):
        move = pltpu.make_async_copy(held, out_ref.at[z], sems.at[z])
        move.start()
        moves.append(move)
    for move in moves:
        move.wait()


def product_kernel(place_ref, *refs):
    same_ref, next_ref, early_ref, out_ref, weight, sems = refs[2 * NX :]
    tokens, depth = refs[0].shape
    step = tokens // NY
    core = place_ref[4]
    odd = lax.rem(place_ref[0], 2)
    half = depth // 2
    loads = []
    for d in range(NX):
        chip = lax.rem(place_ref[3] + (NX - d), NX)
        slab = []
        for c in range(2):
            for i, (ref, at) in enumerate(((same_ref, odd), (next_ref, 1 - odd))):
                rows = pl.ds(pl.multiple_of(c * depth + at * half, half), half)
                slab.append(pltpu.make_async_copy(ref.at[chip * 2 + c], weight.at[d, rows, :], sems.at[d, c, i]))
        for load in slab:
            load.start()
        loads.append(slab)
    own = pl.multiple_of(core * depth, depth)
    far = pl.multiple_of((1 - core) * depth, depth)
    for t in range(NY):
        part = jnp.zeros((step, weight.shape[2]), F32)
        tile = slice(t * step, (t + 1) * step)
        for d in range(NX):
            if t == 0:
                for load in loads[d]:
                    load.wait()
            held = jnp.concatenate([refs[d][tile, :], refs[NX + d][tile, :]], axis=1)
            rows = jnp.concatenate([weight[d, pl.ds(own, depth), :], weight[d, pl.ds(far, depth), :]], axis=0)
            part = part + dot(held, rows, 1, 0)
        part = part.astype(BF16)
        rows = pl.ds(pl.multiple_of(block_of(place_ref, t) * step, step), step)
        for i, h in enumerate(LINE):
            out_ref[i, rows, :] = part[:, h * DH : (h + 1) * DH]


def key_kernel(p0_ref, p1_ref, p2_ref, p3_ref, states_ref):
    for d, ref in enumerate((p0_ref, p1_ref, p2_ref, p3_ref)):
        states_ref[d] = dot(ref[1], ref[2], 0, 0)


def state_kernel(place_ref, p0_ref, p1_ref, p2_ref, p3_ref, part_ref, key_ref, grad_ref, query_ref, copies_ref):
    step = p0_ref.shape[1]
    total_k = jnp.zeros((DH, DH), F32)
    total_q = jnp.zeros((DH, DH), F32)
    for d, ref in enumerate((p0_ref, p1_ref, p2_ref, p3_ref)):
        rows = pl.ds(pl.multiple_of(block_of(place_ref, d) * step, step), step)
        grad = part_ref[0, rows, :].astype(F32)
        for y in range(1, NY):
            grad = grad + part_ref[y, rows, :].astype(F32)
        grad = grad.astype(BF16)
        grad_ref[d] = grad
        query_state = dot(ref[0], grad, 0, 0)
        query_ref[d] = query_state
        total_k = total_k + key_ref[d]
        total_q = total_q + query_state
    for i in range(ZG):
        copies_ref[i, 0] = total_k.astype(BF16)
        copies_ref[i, 1] = total_q.astype(BF16)


def final_kernel(factor, place_ref, p0_ref, p1_ref, p2_ref, p3_ref, grad_ref, key_ref, query_ref, near_ref, far_ref, out_ref):
    step = p0_ref.shape[1]
    inner, outer = place_ref[0], place_ref[1]
    prefix = jnp.zeros((DH, DH), F32)
    suffix = jnp.zeros((DH, DH), F32)
    for i in range(near_ref.shape[0]):
        prefix = prefix + jnp.where(NEAR[i] < inner, near_ref[i, 0].astype(F32), 0.0)
        suffix = suffix + jnp.where(NEAR[i] > inner, near_ref[i, 1].astype(F32), 0.0)
    for i in range(far_ref.shape[0]):
        other = far_ref[i].astype(F32)
        prefix = prefix + jnp.where(FAR[i] < outer, other, 0.0)
        suffix = suffix + jnp.where(FAR[i] > outer, other, 0.0)
    row = lax.broadcasted_iota(jnp.int32, (step, step), 0)
    col = lax.broadcasted_iota(jnp.int32, (step, step), 1)
    lower = row >= col
    upper = row <= col
    for d, ref in enumerate((p0_ref, p1_ref, p2_ref, p3_ref)):
        block = block_of(place_ref, d)
        query, key, value = ref[0], ref[1], ref[2]
        grad = grad_ref[d]
        before, after = prefix, suffix
        for e in range(NY):
            if e != d:
                other = block_of(place_ref, e)
                before = before + jnp.where(other < block, key_ref[e], 0.0)
                after = after + jnp.where(other > block, query_ref[e], 0.0)
        before = before.astype(BF16)
        after = after.astype(BF16)
        scores_grad = jnp.where(lower, dot(grad, value, 1, 1), 0.0).astype(BF16)
        scores_grad_t = jnp.where(upper, dot(value, grad, 1, 1), 0.0).astype(BF16)
        scores_t = jnp.where(upper, dot(key, query, 1, 1), 0.0).astype(BF16)
        grad_q = dot(scores_grad, key, 1, 0) + dot(grad, before, 1, 1)
        grad_k = dot(scores_grad_t, query, 1, 0) + dot(value, after, 1, 1)
        grad_v = dot(scores_t, grad, 1, 0) + dot(key, after, 1, 0)
        to = sum(jnp.where(block == h, i, 0) for i, h in enumerate(LINE))
        out_ref[to, 0] = (factor * grad_q).astype(BF16)
        out_ref[to, 1] = (factor * grad_k).astype(BF16)
        out_ref[to, 2] = (factor * grad_v).astype(BF16)


def unpack_kernel(in_ref, q_ref, k_ref, v_ref):
    for i, h in enumerate(LINE):
        for at, ref in enumerate((q_ref, k_ref, v_ref)):
            ref[:, h * DH : (h + 1) * DH] = in_ref[i, at]


def local(queries, keys, values, grad_out, out_weight):
    step, width = queries.shape
    ctx, tp = lax.axis_size("ctx"), lax.axis_size("tp")
    nz = ctx // NY
    tokens = NY * step
    depth = nz * out_weight.shape[0]
    factor = 1.0 / math.sqrt(step * ctx)
    y_line, z_line, z_near, z_far = groups(ctx)
    at = lax.axis_index("tp")
    here = lax.axis_index("ctx")
    z = here // NY
    place = jnp.stack([z % ZG, z // ZG, here % NY, at // 2, at % 2]).astype(jnp.int32)
    slot = jnp.arange(nz // ZG, dtype=jnp.int32)
    earlier = sum(jnp.where(slot == i, g, 0) for i, g in enumerate(FAR)) < place[1]
    grad_out, place, earlier = lax.optimization_barrier((grad_out, place, earlier))

    copies = call(
        copies_kernel,
        pltpu.HBM((nz // 2,) + out_weight.shape, BF16),
        0,
        2 * depth * width,
        hbm=(0,),
        out_hbm=True,
        scratch=[pltpu.VMEM(out_weight.shape, BF16), pltpu.SemaphoreType.DMA, pltpu.SemaphoreType.DMA((nz // 2,))],
    )(out_weight)
    weight = exchange(copies, z_line)
    beside = lax.ppermute(weight, "ctx", [(i, (i // NY ^ 1) * NY + i % NY) for i in range(ctx)])
    grad_out, copies = lax.optimization_barrier((grad_out, copies))
    turns = {d: [(i, i // NY * NY + (i + d) % NY) for i in range(ctx)] for d in (1, 3, 2)}
    packed = call(
        pack_kernel,
        [shape((4, step, DH))] * NY,
        0,
        8 * step * width * 2,
        smem=(0,),
        hbm=range(1, 5),
        scratch=[
            pltpu.VMEM((step, width), BF16),
            pltpu.VMEM((NY, step, DH), BF16),
            pltpu.SemaphoreType.DMA((NY + 1, 3)),
        ],
    )(place, queries, keys, values, grad_out)
    packed = list(packed)
    for d, turn in turns.items():
        packed[d] = lax.ppermute(packed[d], "ctx", turn)
    mine = call(mine_kernel, shape((tokens, DH)), 0, 4 * tokens * DH)(*packed)
    shares = [mine]
    for d in range(1, NX):
        shares.append(lax.ppermute(mine, "tp", [(t, (t + 2 * d) % tp) for t in range(tp)]))
    swap = [(t, t ^ 1) for t in range(tp)]
    shares = shares + [lax.ppermute(share, "tp", swap) for share in shares]
    key_states = call(
        key_kernel,
        shape((NY, DH, DH), F32),
        4 * tokens * DH * (DH + step),
        2 * 1024 * 1024,
    )(*packed)
    parts = call(
        product_kernel,
        shape((NY, tokens, DH)),
        2 * tokens * depth * width,
        4 * 1024 * 1024,
        smem=(0,),
        hbm=(2 * NX + 1, 2 * NX + 2),
        anywhere=(2 * NX + 3,),
        scratch=[pltpu.VMEM((NX, depth // NX, width), BF16), pltpu.SemaphoreType.DMA((NX, 2, 2))],
    )(place, *shares, weight, beside, key_states)
    parts = exchange(parts, y_line)
    grads, query_states, copies = call(
        state_kernel,
        [shape((NY, step, DH)), shape((NY, DH, DH), F32), shape((ZG, 2, DH, DH))],
        4 * tokens * DH * DH,
        3 * 1024 * 1024,
        smem=(0,),
    )(place, *packed, parts, key_states)
    near = exchange(copies, z_near)
    total = jnp.sum(near.astype(F32), axis=0).astype(BF16)
    far = exchange(jnp.where(earlier[:, None, None], total[1][None], total[0][None]), z_far)
    result = call(
        lambda *refs: final_kernel(factor, *refs),
        shape((NY, 3, step, DH)),
        8 * 2 * tokens * step * DH,
        3 * 1024 * 1024,
        smem=(0,),
    )(place, *packed, grads, key_states, query_states, near, far)
    result = exchange(result, y_line)
    out = shape((step, width))
    return tuple(call(unpack_kernel, [out, out, out], 0, 6 * step * width * 2)(result))


def solution(mesh):
    placed = P("ctx", "tp")
    return jax.shard_map(
        local,
        mesh=mesh,
        in_specs=(placed,) * 5,
        out_specs=(placed,) * 3,
        check_vma=False,
    )
```

```python
import math

import jax
import jax.numpy as jnp
from jax import lax
from jax.experimental import pallas as pl
from jax.experimental.pallas import tpu as pltpu
from jax.sharding import PartitionSpec as P

DH = 128
NY = 4
NX = 4
ZG = 4
LINE = (2, 1, 3, 0)
NEAR = (2, 1, 3, 0)
FAR = (2, 1, 3, 0)
F32 = jnp.float32
BF16 = jnp.bfloat16


def groups(ctx):
    nz = ctx // NY
    y_line = [[z * NY + y for y in LINE] for z in range(nz)]
    z_line = [[z * NY + y for z in range(p, nz, 2)] for p in range(2) for y in range(NY)]
    z_near = [[(g * ZG + i) * NY + y for i in NEAR] for g in range(nz // ZG) for y in range(NY)]
    z_far = [[(g * ZG + i) * NY + y for g in FAR] for i in range(ZG) for y in range(NY)]
    return y_line, z_line, z_near, z_far


def exchange(pieces, group):
    return lax.all_to_all(pieces, "ctx", 0, 0, axis_index_groups=group)


def call(kernel, out_shape, flops, size, smem=(), hbm=(), anywhere=(), scratch=(), out_hbm=False):
    def run(*operands):
        specs = [
            pl.BlockSpec(memory_space=pltpu.SMEM if i in smem else pltpu.HBM if i in hbm else pl.ANY if i in anywhere else pltpu.VMEM)
            for i in range(len(operands))
        ]
        operands = [
            pltpu.with_memory_space_constraint(x, pltpu.HBM) if i in hbm else x for i, x in enumerate(operands)
        ]
        many = isinstance(out_shape, (list, tuple))
        out_specs = [pl.BlockSpec(memory_space=pltpu.VMEM)] * len(out_shape) if many else pl.BlockSpec(memory_space=pltpu.HBM if out_hbm else pltpu.VMEM)
        return pl.pallas_call(
            kernel,
            out_shape=out_shape,
            in_specs=specs,
            out_specs=out_specs,
            scratch_shapes=scratch,
            compiler_params=pltpu.CompilerParams(vmem_limit_bytes=16 * 1024 * 1024),
            cost_estimate=pl.CostEstimate(flops=flops, bytes_accessed=size, transcendentals=0),
        )(*operands)

    return run


def shape(dims, dtype=BF16):
    return jax.ShapeDtypeStruct(dims, dtype)


def dot(a, b, ca, cb):
    return lax.dot_general(a, b, (((ca,), (cb,)), ((), ())), preferred_element_type=F32)


def block_of(place_ref, d):
    return lax.rem(place_ref[2] + (NY - d), NY)


def pack_kernel(place_ref, q_ref, k_ref, v_ref, g_ref, *rest):
    outs, (grad, pieces, sems) = rest[:NY], rest[NY:]
    load = pltpu.make_async_copy(g_ref, grad, sems.at[NY, 0])
    load.start()
    moves = []
    for d, out_ref in enumerate(outs):
        start = pl.multiple_of(lax.rem(place_ref[2] + d, NY) * DH, DH)
        for at, ref in enumerate((q_ref, k_ref, v_ref)):
            move = pltpu.make_async_copy(ref.at[:, pl.ds(start, DH)], out_ref.at[at], sems.at[d, at])
            move.start()
            moves.append(move)
    load.wait()
    rows = grad.shape[1] // (2 * NY)
    for y in range(NY):
        low = grad[:, y * rows : (y + 1) * rows]
        high = grad[:, (NY + y) * rows : (NY + y + 1) * rows]
        pieces[y] = jnp.concatenate([low, high], axis=1)
    for d, out_ref in enumerate(outs):
        out_ref[3] = pieces[lax.rem(place_ref[2] + d, NY)]
    for move in moves:
        move.wait()


def mine_kernel(*refs):
    step = refs[0].shape[1]
    for d in range(NY):
        refs[NY][d * step : (d + 1) * step, :] = refs[d][3]


def copies_kernel(w_ref, out_ref, held, sem, sems):
    load = pltpu.make_async_copy(w_ref, held, sem)
    load.start()
    load.wait()
    moves = []
    for z in range(out_ref.shape[0]):
        move = pltpu.make_async_copy(held, out_ref.at[z], sems.at[z])
        move.start()
        moves.append(move)
    for move in moves:
        move.wait()


def product_kernel(place_ref, *refs):
    same_ref, next_ref, early_ref, out_ref, weight, sems = refs[2 * NX :]
    tokens, depth = refs[0].shape
    step = tokens // NY
    core = place_ref[4]
    odd = lax.rem(place_ref[0], 2)
    half = depth // 2
    loads = []
    for d in range(NX):
        chip = lax.rem(place_ref[3] + (NX - d), NX)
        slab = []
        for c in range(2):
            for i, (ref, at) in enumerate(((same_ref, odd), (next_ref, 1 - odd))):
                rows = pl.ds(pl.multiple_of(c * depth + at * half, half), half)
                slab.append(pltpu.make_async_copy(ref.at[chip * 2 + c], weight.at[d, rows, :], sems.at[d, c, i]))
        for load in slab:
            load.start()
        loads.append(slab)
    own = pl.multiple_of(core * depth, depth)
    far = pl.multiple_of((1 - core) * depth, depth)
    for t in range(NY):
        part = jnp.zeros((step, weight.shape[2]), F32)
        tile = slice(t * step, (t + 1) * step)
        for d in range(NX):
            if t == 0:
                for load in loads[d]:
                    load.wait()
            held = jnp.concatenate([refs[d][tile, :], refs[NX + d][tile, :]], axis=1)
            rows = jnp.concatenate([weight[d, pl.ds(own, depth), :], weight[d, pl.ds(far, depth), :]], axis=0)
            part = part + dot(held, rows, 1, 0)
        part = part.astype(BF16)
        rows = pl.ds(pl.multiple_of(block_of(place_ref, t) * step, step), step)
        for i, h in enumerate(LINE):
            out_ref[i, rows, :] = part[:, h * DH : (h + 1) * DH]


def key_kernel(p0_ref, p1_ref, p2_ref, p3_ref, states_ref):
    for d, ref in enumerate((p0_ref, p1_ref, p2_ref, p3_ref)):
        states_ref[d] = dot(ref[1], ref[2], 0, 0)


def state_kernel(place_ref, p0_ref, p1_ref, p2_ref, p3_ref, part_ref, key_ref, grad_ref, query_ref, copies_ref):
    step = p0_ref.shape[1]
    total_k = jnp.zeros((DH, DH), F32)
    total_q = jnp.zeros((DH, DH), F32)
    for d, ref in enumerate((p0_ref, p1_ref, p2_ref, p3_ref)):
        rows = pl.ds(pl.multiple_of(block_of(place_ref, d) * step, step), step)
        grad = part_ref[0, rows, :].astype(F32)
        for y in range(1, NY):
            grad = grad + part_ref[y, rows, :].astype(F32)
        grad = grad.astype(BF16)
        grad_ref[d] = grad
        query_state = dot(ref[0], grad, 0, 0)
        query_ref[d] = query_state
        total_k = total_k + key_ref[d]
        total_q = total_q + query_state
    for i in range(ZG):
        copies_ref[i, 0] = total_k.astype(BF16)
        copies_ref[i, 1] = total_q.astype(BF16)


def final_kernel(factor, place_ref, p0_ref, p1_ref, p2_ref, p3_ref, grad_ref, key_ref, query_ref, near_ref, far_ref, out_ref):
    step = p0_ref.shape[1]
    inner, outer = place_ref[0], place_ref[1]
    prefix = jnp.zeros((DH, DH), F32)
    suffix = jnp.zeros((DH, DH), F32)
    for i in range(near_ref.shape[0]):
        prefix = prefix + jnp.where(NEAR[i] < inner, near_ref[i, 0].astype(F32), 0.0)
        suffix = suffix + jnp.where(NEAR[i] > inner, near_ref[i, 1].astype(F32), 0.0)
    for i in range(far_ref.shape[0]):
        other = far_ref[i].astype(F32)
        prefix = prefix + jnp.where(FAR[i] < outer, other, 0.0)
        suffix = suffix + jnp.where(FAR[i] > outer, other, 0.0)
    row = lax.broadcasted_iota(jnp.int32, (step, step), 0)
    col = lax.broadcasted_iota(jnp.int32, (step, step), 1)
    lower = row >= col
    upper = row <= col
    for d, ref in enumerate((p0_ref, p1_ref, p2_ref, p3_ref)):
        block = block_of(place_ref, d)
        query, key, value = ref[0], ref[1], ref[2]
        grad = grad_ref[d]
        before, after = prefix, suffix
        for e in range(NY):
            if e != d:
                other = block_of(place_ref, e)
                before = before + jnp.where(other < block, key_ref[e], 0.0)
                after = after + jnp.where(other > block, query_ref[e], 0.0)
        before = before.astype(BF16)
        after = after.astype(BF16)
        scores_grad = jnp.where(lower, dot(grad, value, 1, 1), 0.0).astype(BF16)
        scores_grad_t = jnp.where(upper, dot(value, grad, 1, 1), 0.0).astype(BF16)
        scores_t = jnp.where(upper, dot(key, query, 1, 1), 0.0).astype(BF16)
        grad_q = dot(scores_grad, key, 1, 0) + dot(grad, before, 1, 1)
        grad_k = dot(scores_grad_t, query, 1, 0) + dot(value, after, 1, 1)
        grad_v = dot(scores_t, grad, 1, 0) + dot(key, after, 1, 0)
        to = sum(jnp.where(block == h, i, 0) for i, h in enumerate(LINE))
        out_ref[to, 0] = (factor * grad_q).astype(BF16)
        out_ref[to, 1] = (factor * grad_k).astype(BF16)
        out_ref[to, 2] = (factor * grad_v).astype(BF16)


def unpack_kernel(in_ref, q_ref, k_ref, v_ref):
    for i, h in enumerate(LINE):
        for at, ref in enumerate((q_ref, k_ref, v_ref)):
            ref[:, h * DH : (h + 1) * DH] = in_ref[i, at]


def local(queries, keys, values, grad_out, out_weight):
    step, width = queries.shape
    ctx, tp = lax.axis_size("ctx"), lax.axis_size("tp")
    nz = ctx // NY
    tokens = NY * step
    depth = nz * out_weight.shape[0]
    factor = 1.0 / math.sqrt(step * ctx)
    y_line, z_line, z_near, z_far = groups(ctx)
    at = lax.axis_index("tp")
    here = lax.axis_index("ctx")
    z = here // NY
    place = jnp.stack([z % ZG, z // ZG, here % NY, at // 2, at % 2]).astype(jnp.int32)
    slot = jnp.arange(nz // ZG, dtype=jnp.int32)
    earlier = sum(jnp.where(slot == i, g, 0) for i, g in enumerate(FAR)) < place[1]
    grad_out, place, earlier = lax.optimization_barrier((grad_out, place, earlier))

    copies = call(
        copies_kernel,
        pltpu.HBM((nz // 2,) + out_weight.shape, BF16),
        0,
        2 * depth * width,
        hbm=(0,),
        out_hbm=True,
        scratch=[pltpu.VMEM(out_weight.shape, BF16), pltpu.SemaphoreType.DMA, pltpu.SemaphoreType.DMA((nz // 2,))],
    )(out_weight)
    weight = exchange(copies, z_line)
    beside = lax.ppermute(weight, "ctx", [(i, (i // NY ^ 1) * NY + i % NY) for i in range(ctx)])
    grad_out, copies = lax.optimization_barrier((grad_out, copies))
    turns = {d: [(i, i // NY * NY + (i + d) % NY) for i in range(ctx)] for d in (1, 3, 2)}
    packed = call(
        pack_kernel,
        [shape((4, step, DH))] * NY,
        0,
        8 * step * width * 2,
        smem=(0,),
        hbm=range(1, 5),
        scratch=[
            pltpu.VMEM((step, width), BF16),
            pltpu.VMEM((NY, step, DH), BF16),
            pltpu.SemaphoreType.DMA((NY + 1, 3)),
        ],
    )(place, queries, keys, values, grad_out)
    packed = list(packed)
    for d, turn in turns.items():
        packed[d] = lax.ppermute(packed[d], "ctx", turn)
    mine = call(mine_kernel, shape((tokens, DH)), 0, 4 * tokens * DH)(*packed)
    shares = [mine]
    for d in range(1, NX):
        shares.append(lax.ppermute(mine, "tp", [(t, (t + 2 * d) % tp) for t in range(tp)]))
    swap = [(t, t ^ 1) for t in range(tp)]
    shares = shares + [lax.ppermute(share, "tp", swap) for share in shares]
    key_states = call(
        key_kernel,
        shape((NY, DH, DH), F32),
        4 * tokens * DH * (DH + step),
        2 * 1024 * 1024,
    )(*packed)
    parts = call(
        product_kernel,
        shape((NY, tokens, DH)),
        2 * tokens * depth * width,
        4 * 1024 * 1024,
        smem=(0,),
        hbm=(),
        anywhere=(2 * NX + 1, 2 * NX + 2, 2 * NX + 3),
        scratch=[pltpu.VMEM((NX, depth // NX, width), BF16), pltpu.SemaphoreType.DMA((NX, 2, 2))],
    )(place, *shares, weight, beside, key_states)
    parts = exchange(parts, y_line)
    grads, query_states, copies = call(
        state_kernel,
        [shape((NY, step, DH)), shape((NY, DH, DH), F32), shape((ZG, 2, DH, DH))],
        4 * tokens * DH * DH,
        3 * 1024 * 1024,
        smem=(0,),
    )(place, *packed, parts, key_states)
    near = exchange(copies, z_near)
    total = jnp.sum(near.astype(F32), axis=0).astype(BF16)
    far = exchange(jnp.where(earlier[:, None, None], total[1][None], total[0][None]), z_far)
    result = call(
        lambda *refs: final_kernel(factor, *refs),
        shape((NY, 3, step, DH)),
        8 * 2 * tokens * step * DH,
        3 * 1024 * 1024,
        smem=(0,),
    )(place, *packed, grads, key_states, query_states, near, far)
    result = exchange(result, y_line)
    out = shape((step, width))
    return tuple(call(unpack_kernel, [out, out, out], 0, 6 * step * width * 2)(result))


def solution(mesh):
    placed = P("ctx", "tp")
    return jax.shard_map(
        local,
        mesh=mesh,
        in_specs=(placed,) * 5,
        out_specs=(placed,) * 3,
        check_vma=False,
    )
```
